512 devices in a mesh: dp: 2 (over x_lo), table: 32 (over z, core), tensor: 8 (over x_hi, y).
Axes of the slice: x: 4 (x_hi: 2, x_lo: 2; x = x_hi * 2 + x_lo), y: 4, z: 16, core: 2. Of those that a mesh axis runs over, the one named last changes fastest.
Arguments:
- fetched_table_entries: bfloat16 [64, 1024, 512], P('table', 'dp', 'tensor'), may hold values from -32 to 32
- position_category_number: int32 [64], replicated, may hold values from 0 to 63, each once
- category_shift_vector: float32 [64, 512], P(None, 'tensor'), may hold values from -6 to 6
- asker_matcher_content_matrix: bfloat16 [512, 3, 512], P(None, None, 'tensor'), may hold values from -0.25 to 0.25
- affinity_sharpness: float32 [8], P('tensor'), may hold values from 2 to 8
- mixer_exit_matrix: bfloat16 [512, 512], P('tensor'), may hold values from -0.25 to 0.25
- mixer_rescale_factor: float32 [512], replicated, may hold values from 0.5 to 1.5
- interact_matrix: bfloat16 [512, 512], P(None, 'tensor'), may hold values from -0.25 to 0.25
- interact_offset_vector: float32 [512], P('tensor'), may hold values from -4 to 4
- widening_matrix: bfloat16 [512, 4096], P(None, 'tensor'), may hold values from -0.25 to 0.25
- narrowing_matrix: bfloat16 [4096, 512], P('tensor'), may hold values from -0.09375 to 0.09375
- incoming_cotangent: bfloat16 [1024, 64, 512], P(('dp', 'table')), may hold values from -0.25 to 0.25
Outputs:
- mixed: bfloat16 [1024, 64, 512], P(('dp', 'table'), None, 'tensor')
- grad_cross: float32 [512, 512], P(None, 'tensor')
- grad_bias: float32 [512], P('tensor')
- grad_up: float32 [512, 4096], P(None, 'tensor')
- grad_down: float32 [4096, 512], P('tensor')
The draws below stay inside these ranges and needn't reach their ends.
Inputs may be any that keep to these rules, and one draw needn't show every extreme that they name: `position_category_number`: slots are numbered in the order of the table axis, 64 // 32 to a device; each feature sits in exactly one slot.
All inputs are finite; a program needn't handle non-finite values.
Results may differ from the reference program's by a relative error of at most 0.023.
Values may be sent and summed in bfloat16 or wider, within the bound.
A program may use at most 64 MiB of HBM per device.

```python
import math
import jax
import jax.numpy as jnp
from jax import lax

D = 512
FOCUS_GROUPS = 8
PER_GROUP_SPAN = 64
HID = 4096
F = 64
B_DEV = 16
BATCH = 1024
N_TENSOR = 8


def draw_fetched_table_entries(key, part):
    key = jax.random.fold_in(key, 11)
    key_base, key_rows, key_cols = jax.random.split(key, 3)
    row_scale = jnp.exp(jax.random.uniform(key_rows, (F, BATCH, 1), jnp.float32, -1.15, 1.15))
    col_scale = jnp.exp(jax.random.uniform(key_cols, (1, 1, D), jnp.float32, -1.15, 1.15))
    base = jax.random.normal(key_base, (F, BATCH, D), jnp.float32)
    values = jnp.clip(base * row_scale * col_scale, -32.0, 32.0)
    return values.astype(jnp.bfloat16)


def levels(key, shape, cuts, smallest, top_value):
    factor_of = 1.0
    for dim, blocks in cuts:
        draws = jax.random.uniform(jax.random.fold_in(jax.random.fold_in(key, 6), dim), (blocks,), jnp.float32, smallest / len(cuts), top_value / len(cuts))
        factor_of = factor_of * jnp.repeat(jnp.exp(draws), shape[dim] // blocks).reshape((-1,) + (1,) * (len(shape) - 1 - dim))
    return factor_of


def scatter_about(key, shape, width, most, pieces=(), kind=jnp.bfloat16):
    entries = jax.random.normal(key, shape, jnp.float32) * width
    if len(pieces) > 0:
        entries = levels(key, shape, pieces, -0.22, 0.18) * entries
    return jnp.clip(entries, min=-most, max=most).astype(kind)


def setup_inputs(seed: int = 0) -> dict:
    key_list = jax.random.split(jax.random.key(seed), 13)
    return {
        "fetched_table_entries": draw_fetched_table_entries(jax.random.fold_in(key_list[12], 71), 0),
        "position_category_number": jax.random.permutation(key_list[1], F).astype(jnp.int32),
        "category_shift_vector": scatter_about(key_list[2], (F, D), 1.0, 6.0, ((1, 8),), jnp.float32),
        "asker_matcher_content_matrix": scatter_about(key_list[3], (D, 3, D), D ** -0.5, 0.25, ((2, 8),)),
        "affinity_sharpness": jnp.clip(jnp.exp(math.log(8.0) - 1.3862944 * jax.random.uniform(key_list[4], (FOCUS_GROUPS,), jnp.float32) ** levels(key_list[4], (FOCUS_GROUPS,), ((0, 8),), -0.2, 0.2)), 2.0, 8.0),
        "mixer_exit_matrix": scatter_about(key_list[5], (D, D), D ** -0.5, 0.25, ((0, 8),)),
        "mixer_rescale_factor": jnp.clip(1.0 + 0.1 * jax.random.normal(key_list[6], (D,), jnp.float32), 0.5, 1.5),
        "interact_matrix": scatter_about(key_list[7], (D, D), D ** -0.5, 0.25, ((1, 8),)),
        "interact_offset_vector": scatter_about(key_list[8], (D,), 1.0, 4.0, ((0, 8),), jnp.float32),
        "widening_matrix": scatter_about(key_list[9], (D, HID), D ** -0.5, 0.25, ((1, 8),)),
        "narrowing_matrix": scatter_about(key_list[10], (HID, D), HID ** -0.5, 0.09375, ((0, 8),)),
        "incoming_cotangent": scatter_about(key_list[11], (BATCH, F, D), (4.0 / (BATCH * F) ** 0.5), 0.25, ((0, 64),)),
    }


epsilon = 1e-06

def unit_rows(values):
    return values * lax.rsqrt(lax.optimization_barrier(jnp.mean(values * values, axis=-1, keepdims=True)) + epsilon)

def reference(fetched_table_entries, position_category_number, category_shift_vector, asker_matcher_content_matrix, affinity_sharpness, mixer_exit_matrix, mixer_rescale_factor, interact_matrix, interact_offset_vector, widening_matrix, narrowing_matrix, incoming_cotangent):
    inverse = jnp.argsort(position_category_number).astype(jnp.int32)
    placed = jnp.transpose(jnp.take(fetched_table_entries, inverse, axis=0), (1, 0, 2))
    inputs = (placed.astype(jnp.float32) + category_shift_vector[None]).astype(jnp.bfloat16)
    blocks = BATCH // B_DEV
    row_count = B_DEV * F
    groups = N_TENSOR
    group_width = D // groups
    group_hidden = HID // groups
    inputs = inputs.reshape(blocks, row_count, D)
    cotangents = incoming_cotangent.reshape(blocks, row_count, D)
    projection = asker_matcher_content_matrix.reshape(D, 3 * D)
    shape_four = (B_DEV, F, FOCUS_GROUPS, PER_GROUP_SPAN)
    out_three = mixer_exit_matrix.astype(jnp.float32).reshape(groups, group_width, D)
    down_three = narrowing_matrix.astype(jnp.float32).reshape(groups, group_hidden, D)
    diagonal = jnp.eye(groups, dtype=jnp.float32)[:, None, :, None]

    def step_block(carry, pair):
        input_rows, cotangent = pair
        projected = jnp.dot(input_rows, projection, preferred_element_type=jnp.float32)
        query_unit = unit_rows(projected[:, :D].reshape(shape_four)).astype(jnp.bfloat16)
        key_unit = unit_rows(projected[:, D:2 * D].reshape(shape_four)).astype(jnp.bfloat16)
        value_rows = projected[:, 2 * D:].reshape(shape_four).astype(jnp.bfloat16)
        raw_affinity_logits = jnp.einsum('bihe,bjhe->bhij', query_unit.astype(jnp.float32), key_unit.astype(jnp.float32))
        affinity_matrix = raw_affinity_logits * (affinity_sharpness / PER_GROUP_SPAN)[None, :, None, None]
        exponent = jnp.exp(affinity_matrix)
        attention = (exponent / lax.optimization_barrier(jnp.sum(exponent, axis=-1, keepdims=True))).astype(jnp.bfloat16)
        heads = jnp.einsum('bhij,bjhe->bihe', attention.astype(jnp.float32), value_rows.astype(jnp.float32))
        heads = heads.astype(jnp.bfloat16).reshape(row_count, groups, group_width)
        head_part = jnp.einsum('rgw,gwd->grd', heads.astype(jnp.float32), out_three)
        head_part = head_part.reshape(groups, row_count, groups, group_width)
        own_inputs = input_rows.astype(jnp.float32).reshape(row_count, groups, group_width)
        head_term = (head_part + diagonal * own_inputs[None]).astype(jnp.bfloat16)
        summed = lax.optimization_barrier(jnp.sum(head_term.astype(jnp.float32), axis=0)).reshape(row_count, D)
        normed = (unit_rows(summed) * mixer_rescale_factor).astype(jnp.bfloat16)
        crossed = input_rows.astype(jnp.float32) * (jnp.dot(normed, interact_matrix, preferred_element_type=jnp.float32) + interact_offset_vector) + normed.astype(jnp.float32)
        hidden_pre = jnp.dot(normed, widening_matrix, preferred_element_type=jnp.float32)
        activation = jax.nn.silu(hidden_pre).astype(jnp.bfloat16)
        act_three = activation.astype(jnp.float32).reshape(row_count, groups, group_hidden)
        mlp_term = jnp.einsum('rgk,gkd->grd', act_three, down_three).astype(jnp.bfloat16)
        mixed = (crossed + lax.optimization_barrier(jnp.sum(mlp_term.astype(jnp.float32), axis=0))).astype(jnp.bfloat16)
        grad_down = jnp.dot(activation.T, cotangent, preferred_element_type=jnp.float32)
        back_act = jnp.dot(cotangent, narrowing_matrix.T, preferred_element_type=jnp.float32)
        sigma = jax.nn.sigmoid(hidden_pre)
        slope = (back_act * sigma * (1.0 + hidden_pre * (1.0 - sigma))).astype(jnp.bfloat16)
        grad_up = jnp.dot(normed.T, slope, preferred_element_type=jnp.float32)
        cross_term = cotangent.astype(jnp.float32) * input_rows.astype(jnp.float32)
        grad_bias = lax.optimization_barrier(jnp.sum(cross_term, axis=0))
        grad_cross = jnp.dot(normed.T, cross_term.astype(jnp.bfloat16), preferred_element_type=jnp.float32)
        updated = (carry[0] + grad_cross, carry[1] + grad_bias, carry[2] + grad_up, carry[3] + grad_down)
        return (updated, mixed)
    start = (jnp.zeros((D, D), jnp.float32), jnp.zeros((D,), jnp.float32), jnp.zeros((D, HID), jnp.float32), jnp.zeros((HID, D), jnp.float32))
    totals, mixed = lax.scan(step_block, start, (inputs, cotangents))
    return (mixed.reshape(BATCH, F, D), totals[0], totals[1], totals[2], totals[3])
```

```python
import functools

import jax
import jax.numpy as jnp
from jax import lax
from jax.experimental import pallas as pl
from jax.experimental.pallas import tpu as pltpu
from jax.sharding import PartitionSpec as P

MESH = pl.DeviceIdType.MESH
F32, BF16 = jnp.float32, jnp.bfloat16
EPS = 1e-06

TABLE, TENSOR, Z = 32, 8, 16
CHUNK = 144
CLASS = 4 * CHUNK
HALF = 4 * CLASS
ROWS = 2 * HALF


def nn(a, b):
    return jnp.dot(a, b, preferred_element_type=F32)


def nt(a, b):
    return lax.dot_general(a, b, (((1,), (1,)), ((), ())), preferred_element_type=F32)


def iota(shape, dim):
    return lax.broadcasted_iota(jnp.int32, shape, dim)


def remote(src, dst, send, recv, **device):
    return pltpu.make_async_remote_copy(
        src_ref=src, dst_ref=dst, send_sem=send, recv_sem=recv, device_id=device, device_id_type=MESH
    )


def kernel(
    f_ref, pos_ref, shift_ref, wqkv_ref, sharp_ref, mex_ref, gain_ref, int_ref, off_ref, wup_ref, wdn_ref, cot_ref,
    mixed_ref, gu_ref, gd_ref, gc_ref, gb_ref,
    zs, arr, arrf, xin, xa, own4, all4, own_sharp, all_sharp, xrow, nall, back, wup_t, wdn_t, low, xt, ctt, mlp, rs, cross,
    g32, gb16, crecv, h32, hb16, nr, c32, cb16, fr, fb16, dr, gfin,
    zss, zrs, tss, trs, wss, wrs, css, crs, sss, srs, ass, ars, mss, mrs, gss, grs,
):
    dp = lax.axis_index("dp")
    table = lax.axis_index("table")
    tensor = lax.axis_index("tensor")
    z, core = table // 2, lax.rem(table, 2)
    hi, y = tensor // 4, lax.rem(tensor, 4)
    sibling = table + 1 - 2 * core

    def around(k):
        return lax.rem(table + TABLE + k, TABLE)

    def tensor_at(k):
        return lax.rem(tensor + k, TENSOR)

    barrier = pltpu.get_barrier_semaphore()
    for k in range(1, TABLE):
        pl.semaphore_signal(barrier, inc=1, device_id={"table": around(k)}, device_id_type=MESH)
    for k in range(1, TENSOR):
        pl.semaphore_signal(barrier, inc=1, device_id={"tensor": tensor_at(k)}, device_id_type=MESH)
    pl.semaphore_signal(barrier, inc=1, device_id={"dp": 1 - dp}, device_id_type=MESH)

    zs[...] = f_ref[...].T
    arr[TABLE - 1] = zs[pl.ds(pl.multiple_of(16 * table, 16), 16), :]
    own4[0:3] = wqkv_ref[...]
    own4[3] = mex_ref[...]
    own_sharp[...] = jnp.broadcast_to(sharp_ref[...], own_sharp.shape)
    wup_t[...] = wup_ref[...].T
    wdn_t[...] = wdn_ref[...].T
    low[0:64] = int_ref[...]
    low[64:128] = (iota((64, 512), 1) == 64 * tensor + iota((64, 512), 0)).astype(F32).astype(BF16)
    def backward(i, carry):
        rows = cot_ref[pl.ds(pl.multiple_of(128 * i, 128), 128), :]
        back[i] = nt(wdn_ref[...], rows)
        ctt[i] = nt(low[64:128], rows)
        return carry
    lax.fori_loop(0, TENSOR, backward, 0)
    g32[...] = jnp.zeros_like(g32)

    lane = iota((1, 128), 1)
    left = lane < 64
    hot = (iota((64, 64), 0) == pos_ref[...]).astype(F32).astype(BF16)
    j = iota((64, 64), 1)
    source = 2 * lax.rem(table - lax.rem(j, 32) - 1 + TABLE, TABLE) + j // 32
    place = nn(hot, (iota((64, 64), 0) == source).astype(F32).astype(BF16)).astype(BF16)
    shift = shift_ref[...]
    shift = jnp.concatenate([shift, shift], axis=1)

    pl.semaphore_wait(barrier, TABLE - 1 + TENSOR - 1 + 1)

    to_table = []
    for d in (8, 7, 9, 6, 10, 5, 11, 4, 12, 3, 13, 2, 14, 1, 15, 0):
        for k in (2 * d, 2 * d + 1):
            if k == 0:
                continue
            rows = zs.at[pl.ds(pl.multiple_of(16 * around(k), 16), 16), :]
            copy = remote(rows, arr.at[k - 1], zss.at[k], zrs.at[k], table=around(k))
            copy.start()
            to_table.append(copy)

    pair = pl.ds(2 * core, 2)
    mine = pl.ds(pl.multiple_of(64 * tensor, 64), 64)
    all4[pair, mine, :] = own4[pair]
    all_sharp[tensor] = own_sharp[...]
    weights, sharps = [], []
    for k in range(1, TENSOR):
        copy = remote(own_sharp, all_sharp.at[tensor], sss.at[k], srs.at[k], tensor=tensor_at(k))
        copy.start()
        sharps.append(copy)
    for k in range(1, TENSOR):
        copy = remote(own4.at[pair], all4.at[pair, mine, :], wss.at[k], wrs.at[k], tensor=tensor_at(k))
        copy.start()
        weights.append(copy)

    for copy in to_table:
        copy.wait_recv()
    arrf[...] = arr[...].astype(F32)
    for i in range(TENSOR):
        a, b = arrf[:, 2 * i, :], arrf[:, 2 * i + 1, :]
        even = jnp.where(left, a, pltpu.roll(b, 64, 1))
        odd = jnp.where(left, pltpu.roll(a, 64, 1), b)
        rows = jnp.concatenate([even, odd], axis=0).astype(BF16)
        xin[i] = (nn(place, rows) + shift).astype(BF16)
    to_tensor = []
    for k in range(1, TENSOR):
        copy = remote(xin.at[tensor_at(k)], xa.at[tensor], tss.at[k], trs.at[k], tensor=tensor_at(k))
        copy.start()
        to_tensor.append(copy)
    xa[tensor] = xin[tensor]

    def columns(i, carry):
        t = xin[i].astype(F32).T
        xt[i] = jnp.concatenate([t[0:64], t[64:128]], axis=1)
        return carry
    lax.fori_loop(0, TENSOR, columns, 0)
    term = ctt[...] * xt[...]
    ctt[...] = term
    bias = jnp.sum(jnp.sum(term, axis=0), axis=1, keepdims=True)

    for copy in weights:
        copy.wait_recv()
    over = remote(all4.at[pair], all4.at[pair], css.at[0], crs.at[0], table=sibling)
    over.start()
    for copy in to_tensor + sharps:
        copy.wait_recv()

    for i in range(4):
        a, b = xa[2 * i].astype(F32), xa[2 * i + 1].astype(F32)
        span = slice(128 * i, 128 * i + 128)
        xrow[0:64, span] = jnp.where(left, a, pltpu.roll(b, 64, 1)).astype(BF16)
        xrow[64:128, span] = jnp.where(left, pltpu.roll(a, 64, 1), b).astype(BF16)
    over.wait_recv()

    x = xrow[...]
    same_head = (iota((512, 512), 0) // 64 == iota((512, 512), 1) // 64).astype(F32).astype(BF16)

    def unit(v):
        squares = nn((v * v).astype(BF16), same_head)
        return v * lax.rsqrt(squares * (1.0 / 64) + EPS)

    query = unit(nt(x, all4[0]))
    key = unit(nt(x, all4[1])).astype(BF16)
    value = nt(x, all4[2])
    same_sample = iota((128, 128), 0) // 64 == iota((128, 128), 1) // 64
    heads = []
    for i in range(4):
        span = slice(128 * i, 128 * i + 128)
        q, k, v = query[:, span], key[:, span], value[:, span]
        parts = []
        for s in range(2):
            half = left if s == 0 else jnp.logical_not(left)
            scores = nt(jnp.where(half, q, 0.0).astype(BF16), k) * (all_sharp[2 * i + s, 0:1, :] * (1.0 / 64))
            e = jnp.where(same_sample, jnp.exp(scores), 0.0).astype(BF16)
            o = nn(e, jnp.where(half, v, 1.0).astype(BF16))
            parts.append(o / pltpu.roll(o, 64, 1))
        heads.append(jnp.where(left, parts[0], parts[1]).astype(BF16))
    summed = nn(jnp.concatenate(heads, axis=1), all4[3]) + x.astype(F32)
    mean = jnp.mean(summed * summed, axis=1, keepdims=True)
    nall[tensor] = (summed * lax.rsqrt(mean + EPS) * gain_ref[...]).astype(BF16)

    def relative(r, sign):
        dh, d = r // 4, lax.rem(r, 4)
        dy = d + (d // 2) * (5 - 2 * d)
        return 4 * lax.rem(hi + dh, 2) + lax.rem(y + 4 + sign * dy, 4)

    gathers = []
    for r in range(1, TENSOR):
        copy = remote(nall.at[tensor], nall.at[tensor], ass.at[r], ars.at[r], tensor=relative(r, 1))
        copy.start()
        gathers.append(copy)

    off = jnp.sum(jnp.where(iota((64, 64), 0) == iota((64, 64), 1), off_ref[...], 0.0), axis=1, keepdims=True)

    def chunk(r, carry):
        i = relative(r, -1)

        @pl.when(r > 0)
        def _():
            remote(nall.at[i], nall.at[i], ass.at[r], ars.at[r], tensor=i).wait_recv()

        n = nall[i]
        h = nt(wup_t[...], n)
        sg = 1.0 / (1.0 + jnp.exp(-h))
        act = (h * sg).astype(BF16)
        slope = (back[i] * sg * (1.0 + h * (1.0 - sg))).astype(BF16)
        mlp[i] = nn(wdn_t[...], act).astype(BF16)
        rows = cot_ref[pl.ds(pl.multiple_of(128 * i, 128), 128), :]
        down = nn(act, rows)
        up = nt(n.T, slope)
        side = nn(ctt[i].astype(BF16), n)
        for t in range(4):
            span = slice(128 * t, 128 * t + 128)
            g32[512 * t : 512 * t + 512] += up[:, span]
            g32[2048 + 512 * t : 2560 + 512 * t] += down[:, span]
            g32[4096 + 64 * t : 4160 + 64 * t] += side[:, span]
        c = nt(low[...], n)
        cross[i] = xt[i] * (c[0:64] + off) + c[64:128]
        return carry

    lax.fori_loop(0, TENSOR, chunk, 0)
    g32[4352:4416] = jnp.broadcast_to(bias, (64, 128))

    gb16[...] = g32[...].astype(BF16)
    mine_half = pl.ds(pl.multiple_of(HALF * core, 16), HALF)
    other_half = pl.ds(pl.multiple_of(HALF * (1 - core), 16), HALF)
    cores = remote(gb16.at[other_half], crecv, gss.at[0], grs.at[0], table=sibling)
    cores.start()
    terms = []
    for k in range(1, TENSOR):
        to = tensor_at(k)
        rows = mlp.at[:, pl.ds(pl.multiple_of(64 * to, 64), 64), :]
        copy = remote(rows, rs.at[k - 1], mss.at[k], mrs.at[k], tensor=to)
        copy.start()
        terms.append(copy)
    cores.wait_recv()
    h32[...] = g32[mine_half, :] + crecv[...].astype(F32)
    hb16[...] = h32[...].astype(BF16)

    def class_rows(q):
        return pl.ds(pl.multiple_of(CLASS * lax.rem(q, 4), 16), CLASS)

    near_by = (2, -2, 8 * core - 4)
    near_z = (1, -1, 4 * core - 2)
    near = []
    for i in range(3):
        copy = remote(
            hb16.at[class_rows(z + Z + near_z[i]), :], nr.at[i], gss.at[1 + i], grs.at[1 + i], table=around(near_by[i])
        )
        copy.start()
        near.append(copy)
    for copy in near:
        copy.wait_recv()
    c32[...] = h32[class_rows(z), :] + nr[0].astype(F32) + nr[1].astype(F32) + nr[2].astype(F32)
    cb16[...] = c32[...].astype(BF16)

    def chunk_rows(q):
        return pl.ds(pl.multiple_of(CHUNK * lax.rem(q // 4, 4), 16), CHUNK)

    far = []
    for i, k in enumerate((8, 4, 12)):
        copy = remote(cb16.at[chunk_rows(z + k), :], fr.at[i], gss.at[4 + i], grs.at[4 + i], table=around(2 * k))
        copy.start()
        far.append(copy)
    for copy in terms:
        copy.wait_recv()

    def finish(i, carry):
        own = mlp[i, pl.ds(pl.multiple_of(64 * tensor, 64), 64), :].astype(F32)
        for k in range(1, TENSOR):
            own = own + rs[k - 1, i].astype(F32)
        out = (cross[i] + own).T
        mixed_ref[2 * i] = out[0:64].astype(BF16)
        mixed_ref[2 * i + 1] = out[64:128].astype(BF16)
        return carry

    lax.fori_loop(0, TENSOR, finish, 0)
    for copy in far:
        copy.wait_recv()
    total = c32[chunk_rows(z), :] + fr[0].astype(F32) + fr[1].astype(F32) + fr[2].astype(F32)
    fb16[...] = total.astype(BF16)
    twin = remote(fb16, dr, gss.at[7], grs.at[7], dp=1 - dp)
    twin.start()
    twin.wait_recv()

    base = HALF * core + CLASS * lax.rem(z, 4)
    own_chunk = gfin.at[pl.ds(pl.multiple_of(base + CHUNK * (z // 4), 16), CHUNK), :]
    own_chunk[...] = (fb16[...].astype(F32) + dr[...].astype(F32)).astype(BF16)
    back_far = []
    for i, k in enumerate((8, 4, 12)):
        copy = remote(own_chunk, own_chunk, gss.at[8 + i], grs.at[8 + i], table=around(2 * k))
        copy.start()
        back_far.append(copy)
    for copy in back_far:
        copy.wait_recv()
    own_class = gfin.at[pl.ds(pl.multiple_of(base, 16), CLASS), :]
    back_near = []
    for i in range(3):
        copy = remote(own_class, own_class, gss.at[11 + i], grs.at[11 + i], table=around(near_by[i]))
        copy.start()
        back_near.append(copy)
    across = [remote(own_class, own_class, gss.at[14], grs.at[14], table=sibling)]
    across[0].start()
    for i in range(3):
        back_near[i].wait_recv()
        q = z + Z - near_z[i]
        block = gfin.at[pl.ds(pl.multiple_of(HALF * core + CLASS * lax.rem(q, 4), 16), CLASS), :]
        copy = remote(block, block, gss.at[15 + i], grs.at[15 + i], table=sibling)
        copy.start()
        across.append(copy)
    for copy in across:
        copy.wait_recv()

    for t in range(4):
        span = slice(128 * t, 128 * t + 128)
        gu_ref[:, span] = gfin[512 * t : 512 * t + 512]
        gd_ref[:, span] = gfin[2048 + 512 * t : 2560 + 512 * t]
        gc_ref[:, span] = gfin[4096 + 64 * t : 4160 + 64 * t]
    gb_ref[...] = gfin[4352:4416]

    every = to_table + to_tensor + weights + sharps + [over] + gathers + [cores] + terms + near + far
    for copy in every + [twin] + back_far + back_near + across:
        copy.wait_send()


def body(
    fetched_table_entries,
    position_category_number,
    category_shift_vector,
    asker_matcher_content_matrix,
    affinity_sharpness,
    mixer_exit_matrix,
    mixer_rescale_factor,
    interact_matrix,
    interact_offset_vector,
    widening_matrix,
    narrowing_matrix,
    incoming_cotangent,
):
    vmem = pl.BlockSpec(memory_space=pltpu.VMEM)
    operands = (
        jnp.transpose(fetched_table_entries, (0, 2, 1)).reshape(128, 512),
        position_category_number.reshape(1, 64),
        category_shift_vector,
        jnp.transpose(asker_matcher_content_matrix, (1, 2, 0)),
        affinity_sharpness.reshape(1, 1),
        mixer_exit_matrix,
        mixer_rescale_factor.reshape(1, 512),
        interact_matrix.T,
        interact_offset_vector.reshape(1, 64),
        widening_matrix,
        narrowing_matrix,
        incoming_cotangent.reshape(1024, 512),
    )
    dma = pltpu.SemaphoreType.DMA
    scratch = [
        pltpu.VMEM((512, 128), BF16),
        pltpu.VMEM((32, 16, 128), BF16),
        pltpu.VMEM((32, 16, 128), F32),
        pltpu.VMEM((8, 64, 128), BF16),
        pltpu.VMEM((8, 64, 128), BF16),
        pltpu.VMEM((4, 64, 512), BF16),
        pltpu.VMEM((4, 512, 512), BF16),
        pltpu.VMEM((8, 128), F32),
        pltpu.VMEM((8, 8, 128), F32),
        pltpu.VMEM((128, 512), BF16),
        pltpu.VMEM((8, 128, 512), BF16),
        pltpu.VMEM((8, 512, 128), F32),
        pltpu.VMEM((512, 512), BF16),
        pltpu.VMEM((512, 512), BF16),
        pltpu.VMEM((128, 512), BF16),
        pltpu.VMEM((8, 64, 128), F32),
        pltpu.VMEM((8, 64, 128), F32),
        pltpu.VMEM((8, 512, 128), BF16),
        pltpu.VMEM((7, 8, 64, 128), BF16),
        pltpu.VMEM((8, 64, 128), F32),
        pltpu.VMEM((ROWS, 128), F32),
        pltpu.VMEM((ROWS, 128), BF16),
        pltpu.VMEM((HALF, 128), BF16),
        pltpu.VMEM((HALF, 128), F32),
        pltpu.VMEM((HALF, 128), BF16),
        pltpu.VMEM((3, CLASS, 128), BF16),
        pltpu.VMEM((CLASS, 128), F32),
        pltpu.VMEM((CLASS, 128), BF16),
        pltpu.VMEM((3, CHUNK, 128), BF16),
        pltpu.VMEM((CHUNK, 128), BF16),
        pltpu.VMEM((CHUNK, 128), BF16),
        pltpu.VMEM((ROWS, 128), BF16),
    ]
    for n in (32, 8, 8, 1, 8, 8, 8, 18):
        scratch += [dma((n,)), dma((n,))]
    mixed, up, down, cross, bias = pl.pallas_call(
        kernel,
        name="layer",
        out_shape=(
            jax.ShapeDtypeStruct((16, 64, 64), BF16),
            jax.ShapeDtypeStruct((512, 512), BF16),
            jax.ShapeDtypeStruct((512, 512), BF16),
            jax.ShapeDtypeStruct((64, 512), BF16),
            jax.ShapeDtypeStruct((64, 128), BF16),
        ),
        in_specs=[vmem] * len(operands),
        out_specs=(vmem,) * 5,
        scratch_shapes=scratch,
        compiler_params=pltpu.CompilerParams(
            collective_id=0, has_side_effects=True, vmem_limit_bytes=48 * 2**20
        ),
    )(*operands)
    return mixed, cross.astype(F32).T, bias[:, 0].astype(F32), up.astype(F32), down.astype(F32)


def solution(mesh):
    in_specs = (
        P("table", "dp", "tensor"),
        P(),
        P(None, "tensor"),
        P(None, None, "tensor"),
        P("tensor"),
        P("tensor", None),
        P(),
        P(None, "tensor"),
        P("tensor"),
        P(None, "tensor"),
        P("tensor", None),
        P(("dp", "table"), None, None),
    )
    out_specs = (
        P(("dp", "table"), None, "tensor"),
        P(None, "tensor"),
        P("tensor"),
        P(None, "tensor"),
        P("tensor", None),
    )
    return jax.shard_map(body, mesh=mesh, in_specs=in_specs, out_specs=out_specs, check_vma=False)
```

```python
import functools

import jax
import jax.numpy as jnp
from jax import lax
from jax.experimental import pallas as pl
from jax.experimental.pallas import tpu as pltpu
from jax.sharding import PartitionSpec as P

MESH = pl.DeviceIdType.MESH
F32, BF16 = jnp.float32, jnp.bfloat16
EPS = 1e-06

TABLE, TENSOR, Z = 32, 8, 16
CHUNK = 144
CLASS = 4 * CHUNK
HALF = 4 * CLASS
ROWS = 2 * HALF


def nn(a, b):
    return jnp.dot(a, b, preferred_element_type=F32)


def nt(a, b):
    return lax.dot_general(a, b, (((1,), (1,)), ((), ())), preferred_element_type=F32)


def iota(shape, dim):
    return lax.broadcasted_iota(jnp.int32, shape, dim)


def remote(src, dst, send, recv, **device):
    return pltpu.make_async_remote_copy(
        src_ref=src, dst_ref=dst, send_sem=send, recv_sem=recv, device_id=device, device_id_type=MESH
    )


def kernel(
    f_hbm, pos_hbm, shift_hbm, wqkv_hbm, sharp_hbm, mex_hbm, gain_hbm, int_hbm, off_hbm, wup_hbm, wdn_hbm, cot_hbm,
    mixed_ref, gfin,
    f_ref, pos_ref, shift_ref, gain_ref, off_ref, sharp_ref, wup_ref, wdn_ref, cot_ref,
    zs, arr, arrf, xin, xa, own4, all4, own_sharp, all_sharp, xrow, nall, back, wup_t, wdn_t, low, xt, ctt, mlp, rs, cross,
    g32, gb16, crecv, hb16, nr, c32, cb16, fr, fb16, dr,
    zss, zrs, tss, trs, wss, wrs, css, crs, sss, srs, ass, ars, mss, mrs, gss, grs, los,
):
    loads = []
    for hbm, ref in (
        (f_hbm, f_ref), (wup_hbm, wup_ref), (wdn_hbm, wdn_ref), (int_hbm, low.at[0:64]), (cot_hbm, cot_ref),
        (wqkv_hbm, own4.at[0:3]), (mex_hbm, own4.at[3]), (pos_hbm, pos_ref), (shift_hbm, shift_ref),
        (gain_hbm, gain_ref), (off_hbm, off_ref), (sharp_hbm, sharp_ref),
    ):
        copy = pltpu.make_async_copy(hbm, ref, los.at[len(loads)])
        copy.start()
        loads.append(copy)
    dp = lax.axis_index("dp")
    table = lax.axis_index("table")
    tensor = lax.axis_index("tensor")
    z, core = table // 2, lax.rem(table, 2)
    hi, y = tensor // 4, lax.rem(tensor, 4)
    sibling = table + 1 - 2 * core

    def around(k):
        return lax.rem(table + TABLE + k, TABLE)

    def tensor_at(k):
        return lax.rem(tensor + k, TENSOR)

    barrier = pltpu.get_barrier_semaphore()
    for k in range(1, TABLE):
        pl.semaphore_signal(barrier, inc=1, device_id={"table": around(k)}, device_id_type=MESH)
    for k in range(1, TENSOR):
        pl.semaphore_signal(barrier, inc=1, device_id={"tensor": tensor_at(k)}, device_id_type=MESH)
    pl.semaphore_signal(barrier, inc=1, device_id={"dp": 1 - dp}, device_id_type=MESH)

    loads[0].wait()
    zs[...] = f_ref[...].T
    arr[TABLE - 1] = zs[pl.ds(pl.multiple_of(16 * table, 16), 16), :]
    loads[1].wait()
    wup_t[...] = wup_ref[...].T
    loads[2].wait()
    wdn_t[...] = wdn_ref[...].T
    for copy in loads[3:]:
        copy.wait()
    own_sharp[...] = jnp.broadcast_to(sharp_ref[...], own_sharp.shape)
    low[64:128] = (iota((64, 512), 1) == 64 * tensor + iota((64, 512), 0)).astype(F32).astype(BF16)
    def backward(i, carry):
        rows = cot_ref[pl.ds(pl.multiple_of(128 * i, 128), 128), :]
        back[i] = nt(wdn_ref[...], rows)
        ctt[i] = nt(low[64:128], rows)
        return carry
    lax.fori_loop(0, TENSOR, backward, 0)
    g32[...] = jnp.zeros_like(g32)

    lane = iota((1, 128), 1)
    left = lane < 64
    hot = (iota((64, 64), 0) == pos_ref[...]).astype(F32).astype(BF16)
    j = iota((64, 64), 1)
    source = 2 * lax.rem(table - lax.rem(j, 32) - 1 + TABLE, TABLE) + j // 32
    place = nn(hot, (iota((64, 64), 0) == source).astype(F32).astype(BF16)).astype(BF16)
    shift = shift_ref[...]
    shift = jnp.concatenate([shift, shift], axis=1)

    pl.semaphore_wait(barrier, TABLE - 1 + TENSOR - 1 + 1)

    to_table = []
    for d in (8, 7, 9, 6, 10, 5, 11, 4, 12, 3, 13, 2, 14, 1, 15, 0):
        for k in (2 * d, 2 * d + 1):
            if k == 0:
                continue
            rows = zs.at[pl.ds(pl.multiple_of(16 * around(k), 16), 16), :]
            copy = remote(rows, arr.at[k - 1], zss.at[k], zrs.at[k], table=around(k))
            copy.start()
            to_table.append(copy)

    pair = pl.ds(2 * core, 2)
    mine = pl.ds(pl.multiple_of(64 * tensor, 64), 64)
    all4[pair, mine, :] = own4[pair]
    all_sharp[tensor] = own_sharp[...]
    weights, sharps = [], []
    for k in range(1, TENSOR):
        copy = remote(own_sharp, all_sharp.at[tensor], sss.at[k], srs.at[k], tensor=tensor_at(k))
        copy.start()
        sharps.append(copy)
    for k in range(1, TENSOR):
        copy = remote(own4.at[pair], all4.at[pair, mine, :], wss.at[k], wrs.at[k], tensor=tensor_at(k))
        copy.start()
        weights.append(copy)

    for copy in to_table:
        copy.wait_recv()
    arrf[...] = arr[...].astype(F32)
    for i in range(TENSOR):
        a, b = arrf[:, 2 * i, :], arrf[:, 2 * i + 1, :]
        even = jnp.where(left, a, pltpu.roll(b, 64, 1))
        odd = jnp.where(left, pltpu.roll(a, 64, 1), b)
        rows = jnp.concatenate([even, odd], axis=0).astype(BF16)
        xin[i] = (nn(place, rows) + shift).astype(BF16)
    to_tensor = []
    for k in range(1, TENSOR):
        copy = remote(xin.at[tensor_at(k)], xa.at[tensor], tss.at[k], trs.at[k], tensor=tensor_at(k))
        copy.start()
        to_tensor.append(copy)
    xa[tensor] = xin[tensor]

    def columns(i, carry):
        t = xin[i].astype(F32).T
        xt[i] = jnp.concatenate([t[0:64], t[64:128]], axis=1)
        return carry
    lax.fori_loop(0, TENSOR, columns, 0)
    term = ctt[...] * xt[...]
    ctt[...] = term
    bias = jnp.sum(jnp.sum(term, axis=0), axis=1, keepdims=True)

    for copy in weights:
        copy.wait_recv()
    over = remote(all4.at[pair], all4.at[pair], css.at[0], crs.at[0], table=sibling)
    over.start()
    for copy in to_tensor + sharps:
        copy.wait_recv()

    for i in range(4):
        a, b = xa[2 * i].astype(F32), xa[2 * i + 1].astype(F32)
        span = slice(128 * i, 128 * i + 128)
        xrow[0:64, span] = jnp.where(left, a, pltpu.roll(b, 64, 1)).astype(BF16)
        xrow[64:128, span] = jnp.where(left, pltpu.roll(a, 64, 1), b).astype(BF16)
    over.wait_recv()

    x = xrow[...]
    same_head = (iota((512, 512), 0) // 64 == iota((512, 512), 1) // 64).astype(F32).astype(BF16)

    def unit(v):
        squares = nn((v * v).astype(BF16), same_head)
        return v * lax.rsqrt(squares * (1.0 / 64) + EPS)

    query = unit(nt(x, all4[0]))
    key = unit(nt(x, all4[1])).astype(BF16)
    value = nt(x, all4[2])
    same_sample = iota((128, 128), 0) // 64 == iota((128, 128), 1) // 64
    heads = []
    for i in range(4):
        span = slice(128 * i, 128 * i + 128)
        q, k, v = query[:, span], key[:, span], value[:, span]
        parts = []
        for s in range(2):
            half = left if s == 0 else jnp.logical_not(left)
            scores = nt(jnp.where(half, q, 0.0).astype(BF16), k) * (all_sharp[2 * i + s, 0:1, :] * (1.0 / 64))
            e = jnp.where(same_sample, jnp.exp(scores), 0.0).astype(BF16)
            o = nn(e, jnp.where(half, v, 1.0).astype(BF16))
            parts.append(o / pltpu.roll(o, 64, 1))
        heads.append(jnp.where(left, parts[0], parts[1]).astype(BF16))
    summed = nn(jnp.concatenate(heads, axis=1), all4[3]) + x.astype(F32)
    mean = jnp.mean(summed * summed, axis=1, keepdims=True)
    nall[tensor] = (summed * lax.rsqrt(mean + EPS) * gain_ref[...]).astype(BF16)

    def relative(r, sign):
        dh, d = r // 4, lax.rem(r, 4)
        dy = d + (d // 2) * (5 - 2 * d)
        return 4 * lax.rem(hi + dh, 2) + lax.rem(y + 4 + sign * dy, 4)

    gathers = []
    for r in range(1, TENSOR):
        copy = remote(nall.at[tensor], nall.at[tensor], ass.at[r], ars.at[r], tensor=relative(r, 1))
        copy.start()
        gathers.append(copy)

    off = jnp.sum(jnp.where(iota((64, 64), 0) == iota((64, 64), 1), off_ref[...], 0.0), axis=1, keepdims=True)

    def chunk(r, carry):
        i = relative(r, -1)

        @pl.when(r > 0)
        def _():
            remote(nall.at[i], nall.at[i], ass.at[r], ars.at[r], tensor=i).wait_recv()

        n = nall[i]
        h = nt(wup_t[...], n)
        sg = 1.0 / (1.0 + jnp.exp(-h))
        act = (h * sg).astype(BF16)
        slope = (back[i] * sg * (1.0 + h * (1.0 - sg))).astype(BF16)
        mlp[i] = nn(wdn_t[...], act).astype(BF16)
        rows = cot_ref[pl.ds(pl.multiple_of(128 * i, 128), 128), :]
        down = nn(act, rows)
        up = nt(n.T, slope)
        side = nn(ctt[i].astype(BF16), n)
        for t in range(4):
            span = slice(128 * t, 128 * t + 128)
            g32[512 * t : 512 * t + 512] += up[:, span]
            g32[2048 + 512 * t : 2560 + 512 * t] += down[:, span]
            g32[4096 + 64 * t : 4160 + 64 * t] += side[:, span]
        c = nt(low[...], n)
        cross[i] = xt[i] * (c[0:64] + off) + c[64:128]
        return carry

    lax.fori_loop(0, TENSOR, chunk, 0)
    g32[4352:4416] = jnp.broadcast_to(bias, (64, 128))

    gb16[...] = g32[...].astype(BF16)

    def owned(zz):
        zz = lax.rem(zz + 2 * Z, Z)
        return pl.multiple_of(CLASS * lax.rem(zz, 4) + CHUNK * (zz // 4), 16)

    def rows_of(c, zz):
        return pl.ds(pl.multiple_of(HALF * c + owned(zz), 16), CHUNK)

    steps = (8, 4, 12, 0)
    cores = []
    for k in steps:
        for d in (1, -1, 2 - 4 * core, 0):
            n = len(cores)
            copy = remote(
                gb16.at[rows_of(1 - core, z + d + k), :], crecv.at[n], css.at[1 + n], crs.at[1 + n], table=sibling
            )
            copy.start()
            cores.append(copy)
    terms = []
    for k in range(1, TENSOR):
        to = tensor_at(k)
        rows = mlp.at[:, pl.ds(pl.multiple_of(64 * to, 64), 64), :]
        copy = remote(rows, rs.at[k - 1], mss.at[k], mrs.at[k], tensor=to)
        copy.start()
        terms.append(copy)

    near_z = (1, -1, 4 * core - 2)
    near_by = (2, -2, 8 * core - 4)
    near = []
    for s, k in enumerate(steps):
        for i in range(3):
            n = 4 * s + i
            cores[n].wait_recv()
            part = g32[rows_of(core, z + near_z[i] + k), :] + crecv[n].astype(F32)
            hb16[3 * s + i] = part.astype(BF16)
            copy = remote(hb16.at[3 * s + i], nr.at[3 * s + i], gss.at[3 * s + i], grs.at[3 * s + i], table=around(near_by[i]))
            copy.start()
            near.append(copy)
    far = []
    for s, k in enumerate(steps):
        n = 4 * s + 3
        cores[n].wait_recv()
        total = g32[rows_of(core, z + k), :] + crecv[n].astype(F32)
        for i in range(3):
            near[3 * s + i].wait_recv()
            total = total + nr[3 * s + i].astype(F32)
        if k:
            cb16[s] = total.astype(BF16)
            copy = remote(cb16.at[s], fr.at[s], gss.at[12 + s], grs.at[12 + s], table=around(2 * k))
            copy.start()
            far.append(copy)
        else:
            c32[...] = total
    for copy in far:
        copy.wait_recv()
    total = c32[...] + fr[0].astype(F32) + fr[1].astype(F32) + fr[2].astype(F32)
    fb16[...] = total.astype(BF16)
    twin = remote(fb16, dr, gss.at[15], grs.at[15], dp=1 - dp)
    twin.start()
    twin.wait_recv()
    gfin[rows_of(core, z), :] = (fb16[...].astype(F32) + dr[...].astype(F32)).astype(BF16)

    back_far, back_near, across = [], [], []

    def same(zz, s, device):
        block = gfin.at[rows_of(core, zz), :]
        copy = remote(block, block, gss.at[s], grs.at[s], table=device)
        copy.start()
        return copy

    def hand_on(zz, s):
        for i in range(3):
            back_near.append(same(zz, 19 + 3 * s + i, around(near_by[i])))
        across.append(same(zz, 31 + s, sibling))

    for s in range(3):
        back_far.append(same(z, 16 + s, around(2 * steps[s])))
    hand_on(z, 3)

    for copy in terms:
        copy.wait_recv()

    def finish(i, carry):
        own = mlp[i, pl.ds(pl.multiple_of(64 * tensor, 64), 64), :].astype(F32)
        for k in range(1, TENSOR):
            own = own + rs[k - 1, i].astype(F32)
        out = (cross[i] + own).T
        mixed_ref[2 * i] = out[0:64].astype(BF16)
        mixed_ref[2 * i + 1] = out[64:128].astype(BF16)
        return carry

    lax.fori_loop(0, TENSOR, finish, 0)
    for s in (1, 2, 0):
        back_far[s].wait_recv()
        hand_on(z - steps[s], s)
    for order, s in enumerate((3, 1, 2, 0)):
        for i in range(3):
            back_near[3 * order + i].wait_recv()
            across.append(same(z - near_z[i] - steps[s], 35 + 3 * s + i, sibling))
    for copy in across:
        copy.wait_recv()

    every = to_table + to_tensor + weights + sharps + [over] + gathers + cores + terms + near + far
    for copy in every + [twin] + back_far + back_near + across:
        copy.wait_send()


def write_out(mixed_ref, g_ref, mixed_hbm, gc_hbm, gb_hbm, gu_hbm, gd_hbm, gc, gb, gu, gd, sems):
    copies = []

    def send(ref, hbm):
        copies.append(pltpu.make_async_copy(ref, hbm, sems.at[len(copies)]))
        copies[-1].start()

    send(mixed_ref, mixed_hbm)
    for t in range(4):
        gu[:, 128 * t : 128 * t + 128] = g_ref[512 * t : 512 * t + 512].astype(F32)
    send(gu, gu_hbm)
    for t in range(4):
        gd[:, 128 * t : 128 * t + 128] = g_ref[2048 + 512 * t : 2560 + 512 * t].astype(F32)
    send(gd, gd_hbm)
    for t in range(4):
        gc[:, 128 * t : 128 * t + 128] = g_ref[4096 + 64 * t : 4160 + 64 * t].astype(F32)
    send(gc, gc_hbm)
    gb[...] = g_ref[4352:4416].astype(F32).T[0:1]
    send(gb, gb_hbm)
    for copy in copies:
        copy.wait()


def body(
    fetched_table_entries,
    position_category_number,
    category_shift_vector,
    asker_matcher_content_matrix,
    affinity_sharpness,
    mixer_exit_matrix,
    mixer_rescale_factor,
    interact_matrix,
    interact_offset_vector,
    widening_matrix,
    narrowing_matrix,
    incoming_cotangent,
):
    vmem = pl.BlockSpec(memory_space=pltpu.VMEM)
    operands = (
        jnp.transpose(fetched_table_entries, (0, 2, 1)).reshape(128, 512),
        position_category_number.reshape(1, 64),
        category_shift_vector,
        jnp.transpose(asker_matcher_content_matrix, (1, 2, 0)),
        affinity_sharpness.reshape(1, 1),
        mixer_exit_matrix,
        mixer_rescale_factor.reshape(1, 512),
        interact_matrix.T,
        interact_offset_vector.reshape(1, 64),
        widening_matrix,
        narrowing_matrix,
        incoming_cotangent.reshape(1024, 512),
    )
    dma = pltpu.SemaphoreType.DMA
    scratch = [
        pltpu.VMEM((128, 512), BF16),
        pltpu.VMEM((1, 64), jnp.int32),
        pltpu.VMEM((64, 64), F32),
        pltpu.VMEM((1, 512), F32),
        pltpu.VMEM((1, 64), F32),
        pltpu.VMEM((1, 1), F32),
        pltpu.VMEM((512, 512), BF16),
        pltpu.VMEM((512, 512), BF16),
        pltpu.VMEM((1024, 512), BF16),
        pltpu.VMEM((512, 128), BF16),
        pltpu.VMEM((32, 16, 128), BF16),
        pltpu.VMEM((32, 16, 128), F32),
        pltpu.VMEM((8, 64, 128), BF16),
        pltpu.VMEM((8, 64, 128), BF16),
        pltpu.VMEM((4, 64, 512), BF16),
        pltpu.VMEM((4, 512, 512), BF16),
        pltpu.VMEM((8, 128), F32),
        pltpu.VMEM((8, 8, 128), F32),
        pltpu.VMEM((128, 512), BF16),
        pltpu.VMEM((8, 128, 512), BF16),
        pltpu.VMEM((8, 512, 128), F32),
        pltpu.VMEM((512, 512), BF16),
        pltpu.VMEM((512, 512), BF16),
        pltpu.VMEM((128, 512), BF16),
        pltpu.VMEM((8, 64, 128), F32),
        pltpu.VMEM((8, 64, 128), F32),
        pltpu.VMEM((8, 512, 128), BF16),
        pltpu.VMEM((7, 8, 64, 128), BF16),
        pltpu.VMEM((8, 64, 128), F32),
        pltpu.VMEM((ROWS, 128), F32),
        pltpu.VMEM((ROWS, 128), BF16),
        pltpu.VMEM((16, CHUNK, 128), BF16),
        pltpu.VMEM((12, CHUNK, 128), BF16),
        pltpu.VMEM((12, CHUNK, 128), BF16),
        pltpu.VMEM((CHUNK, 128), F32),
        pltpu.VMEM((3, CHUNK, 128), BF16),
        pltpu.VMEM((3, CHUNK, 128), BF16),
        pltpu.VMEM((CHUNK, 128), BF16),
        pltpu.VMEM((CHUNK, 128), BF16),
    ]
    for n in (32, 8, 8, 17, 8, 8, 8, 47):
        scratch += [dma((n,)), dma((n,))]
    scratch.append(dma((12,)))
    mixed, grads = pl.pallas_call(
        kernel,
        name="layer",
        out_shape=(pltpu.VMEM((16, 64, 64), BF16), pltpu.VMEM((ROWS, 128), BF16)),
        in_specs=[pl.BlockSpec(memory_space=pltpu.HBM)] * len(operands),
        out_specs=(vmem,) * 2,
        scratch_shapes=scratch,
        compiler_params=pltpu.CompilerParams(
            collective_id=0, has_side_effects=True, vmem_limit_bytes=58 * 2**20
        ),
    )(*operands)
    hbm = pl.BlockSpec(memory_space=pltpu.HBM)
    mixed, cross, bias, up, down = pl.pallas_call(
        write_out,
        name="write_out",
        out_shape=(
            jax.ShapeDtypeStruct((16, 64, 64), BF16),
            jax.ShapeDtypeStruct((64, 512), F32),
            jax.ShapeDtypeStruct((1, 64), F32),
            jax.ShapeDtypeStruct((512, 512), F32),
            jax.ShapeDtypeStruct((512, 512), F32),
        ),
        in_specs=(vmem,) * 2,
        out_specs=(hbm,) * 5,
        scratch_shapes=[
            pltpu.VMEM((64, 512), F32),
            pltpu.VMEM((1, 64), F32),
            pltpu.VMEM((512, 512), F32),
            pltpu.VMEM((512, 512), F32),
            dma((5,)),
        ],
        compiler_params=pltpu.CompilerParams(vmem_limit_bytes=16 * 2**20),
    )(mixed, grads)
    return mixed, cross.T, bias.reshape(64), up, down


def solution(mesh):
    in_specs = (
        P("table", "dp", "tensor"),
        P(),
        P(None, "tensor"),
        P(None, None, "tensor"),
        P("tensor"),
        P("tensor", None),
        P(),
        P(None, "tensor"),
        P("tensor"),
        P(None, "tensor"),
        P("tensor", None),
        P(("dp", "table"), None, None),
    )
    out_specs = (
        P(("dp", "table"), None, "tensor"),
        P(None, "tensor"),
        P("tensor"),
        P(None, "tensor"),
        P("tensor", None),
    )
    return jax.shard_map(body, mesh=mesh, in_specs=in_specs, out_specs=out_specs, check_vma=False)
```

```python
import functools

import jax
import jax.numpy as jnp
from jax import lax
from jax.experimental import pallas as pl
from jax.experimental.pallas import tpu as pltpu
from jax.sharding import PartitionSpec as P

MESH = pl.DeviceIdType.MESH
F32, BF16 = jnp.float32, jnp.bfloat16
EPS = 1e-06

TABLE, TENSOR, Z = 32, 8, 16
CHUNK = 144
CLASS = 4 * CHUNK
HALF = 4 * CLASS
ROWS = 2 * HALF
FAR_FIRST = [k for d in (8, 7, 9, 6, 10, 5, 11, 4, 12, 3, 13, 2, 14, 1, 15, 0) for k in (2 * d, 2 * d + 1) if k]


def nn(a, b):
    return jnp.dot(a, b, preferred_element_type=F32)


def nt(a, b):
    return lax.dot_general(a, b, (((1,), (1,)), ((), ())), preferred_element_type=F32)


def iota(shape, dim):
    return lax.broadcasted_iota(jnp.int32, shape, dim)


def remote(src, dst, send, recv, **device):
    return pltpu.make_async_remote_copy(
        src_ref=src, dst_ref=dst, send_sem=send, recv_sem=recv, device_id=device, device_id_type=MESH
    )


def kernel(
    f_hbm, pos_hbm, shift_hbm, wqkv_hbm, sharp_hbm, mex_hbm, gain_hbm, int_hbm, off_hbm, wup_hbm, wdn_hbm, cot_hbm,
    mixed_ref, gfin,
    f_ref, pos_ref, shift_ref, gain_ref, off_ref, sharp_ref, wup_ref, wdn_ref, cot_ref,
    zs, arr, arrf, xin, xa, own4, all4, own_sharp, all_sharp, xrow, nall, back, wup_t, wdn_t, low, xt, ctt, mlp, rs, cross,
    g32, gb16, crecv, hb16, nr, c32, cb16, fr, fb16, dr,
    zss, zrs, tss, trs, wss, wrs, css, crs, sss, srs, ass, ars, mss, mrs, gss, grs, los,
):
    dp = lax.axis_index("dp")
    table = lax.axis_index("table")
    tensor = lax.axis_index("tensor")
    z, core = table // 2, lax.rem(table, 2)
    hi, y = tensor // 4, lax.rem(tensor, 4)
    sibling = table + 1 - 2 * core

    def around(k):
        return lax.rem(table + TABLE + k, TABLE)

    def tensor_at(k):
        return lax.rem(tensor + k, TENSOR)

    barrier = pltpu.get_barrier_semaphore()
    for k in FAR_FIRST:
        pl.semaphore_signal(barrier, inc=1, device_id={"table": around(k)}, device_id_type=MESH)
    for k in range(1, TENSOR):
        pl.semaphore_signal(barrier, inc=1, device_id={"tensor": tensor_at(k)}, device_id_type=MESH)
    pl.semaphore_signal(barrier, inc=1, device_id={"dp": 1 - dp}, device_id_type=MESH)

    loads = []
    for hbm, ref in (
        (f_hbm, f_ref), (wup_hbm, wup_ref), (wdn_hbm, wdn_ref), (int_hbm, low.at[0:64]), (cot_hbm, cot_ref),
        (wqkv_hbm, own4.at[0:3]), (mex_hbm, own4.at[3]), (pos_hbm, pos_ref), (shift_hbm, shift_ref),
        (gain_hbm, gain_ref), (off_hbm, off_ref), (sharp_hbm, sharp_ref),
    ):
        copy = pltpu.make_async_copy(hbm, ref, los.at[len(loads)])
        copy.start()
        loads.append(copy)

    loads[0].wait()
    zs[...] = f_ref[...].T
    arr[TABLE - 1] = zs[pl.ds(pl.multiple_of(16 * table, 16), 16), :]
    loads[1].wait()
    wup_t[...] = wup_ref[...].T
    loads[2].wait()
    wdn_t[...] = wdn_ref[...].T
    for copy in loads[3:]:
        copy.wait()
    own_sharp[...] = jnp.broadcast_to(sharp_ref[...], own_sharp.shape)
    low[64:128] = (iota((64, 512), 1) == 64 * tensor + iota((64, 512), 0)).astype(F32).astype(BF16)
    def backward(i, carry):
        rows = cot_ref[pl.ds(pl.multiple_of(128 * i, 128), 128), :]
        back[i] = nt(wdn_ref[...], rows)
        ctt[i] = nt(low[64:128], rows)
        return carry
    lax.fori_loop(0, TENSOR, backward, 0)
    g32[...] = jnp.zeros_like(g32)

    lane = iota((1, 128), 1)
    left = lane < 64
    hot = (iota((64, 64), 0) == pos_ref[...]).astype(F32).astype(BF16)
    j = iota((64, 64), 1)
    source = 2 * lax.rem(table - lax.rem(j, 32) - 1 + TABLE, TABLE) + j // 32
    place = nn(hot, (iota((64, 64), 0) == source).astype(F32).astype(BF16)).astype(BF16)
    shift = shift_ref[...]
    shift = jnp.concatenate([shift, shift], axis=1)

    pl.semaphore_wait(barrier, TABLE - 1 + TENSOR - 1 + 1)

    ring = (1, 3, 2)

    def at(h, k):
        return 4 * lax.rem(hi + h, 2) + lax.rem(y + 4 + k, 4)

    def shard(block, count, owner):
        return all4.at[pl.ds(2 * core + block, count), pl.ds(pl.multiple_of(64 * owner, 64), 64), :]

    all4[pl.ds(2 * core, 2), pl.ds(pl.multiple_of(64 * tensor, 64), 64), :] = own4[pl.ds(2 * core, 2)]
    all_sharp[tensor] = own_sharp[...]
    weights, sharps = [], []

    def spread(block, count, owner, n, to):
        copy = remote(shard(block, count, owner), shard(block, count, owner), wss.at[n], wrs.at[n], tensor=to)
        copy.start()
        weights.append(copy)

    spread(0, 2, tensor, 0, at(1, 0))
    for k in ring:
        spread(0, 2, tensor, k, at(0, k))

    to_table = []
    for k in FAR_FIRST:
        rows = zs.at[pl.ds(pl.multiple_of(16 * around(k), 16), 16), :]
        copy = remote(rows, arr.at[k - 1], zss.at[k], zrs.at[k], table=around(k))
        copy.start()
        to_table.append(copy)
    for k in range(1, TENSOR):
        copy = remote(own_sharp, all_sharp.at[tensor], sss.at[k], srs.at[k], tensor=tensor_at(k))
        copy.start()
        sharps.append(copy)

    over = []

    def hand_over(owner):
        n = len(over)
        copy = remote(shard(0, 2, owner), shard(0, 2, owner), css.at[n], crs.at[n], table=sibling)
        copy.start()
        over.append(copy)

    hand_over(tensor)
    weights[0].wait_recv()
    for k in ring:
        spread(0, 1, at(1, 0), 4 + k, at(0, k))
    hand_over(at(1, 0))
    for n, k in enumerate(ring):
        weights[1 + n].wait_recv()
        spread(1, 1, at(0, -k), 8 + k, at(1, 0))
        hand_over(at(0, -k))

    for copy in to_table:
        copy.wait_recv()
    arrf[...] = arr[...].astype(F32)
    for i in range(TENSOR):
        a, b = arrf[:, 2 * i, :], arrf[:, 2 * i + 1, :]
        even = jnp.where(left, a, pltpu.roll(b, 64, 1))
        odd = jnp.where(left, pltpu.roll(a, 64, 1), b)
        rows = jnp.concatenate([even, odd], axis=0).astype(BF16)
        xin[i] = (nn(place, rows) + shift).astype(BF16)
    to_tensor = []
    for k in range(1, TENSOR):
        copy = remote(xin.at[tensor_at(k)], xa.at[tensor], tss.at[k], trs.at[k], tensor=tensor_at(k))
        copy.start()
        to_tensor.append(copy)
    xa[tensor] = xin[tensor]

    def columns(i, carry):
        t = xin[i].astype(F32).T
        xt[i] = jnp.concatenate([t[0:64], t[64:128]], axis=1)
        return carry
    lax.fori_loop(0, TENSOR, columns, 0)
    term = ctt[...] * xt[...]
    ctt[...] = term
    bias = jnp.sum(jnp.sum(term, axis=0), axis=1, keepdims=True)

    for n, k in enumerate(ring):
        weights[4 + n].wait_recv()
        weights[7 + n].wait_recv()
        hand_over(at(1, -k))
    for copy in to_tensor + sharps:
        copy.wait_recv()

    for i in range(4):
        a, b = xa[2 * i].astype(F32), xa[2 * i + 1].astype(F32)
        span = slice(128 * i, 128 * i + 128)
        xrow[0:64, span] = jnp.where(left, a, pltpu.roll(b, 64, 1)).astype(BF16)
        xrow[64:128, span] = jnp.where(left, pltpu.roll(a, 64, 1), b).astype(BF16)
    for copy in over:
        copy.wait_recv()

    x = xrow[...]
    same_head = (iota((512, 512), 0) // 64 == iota((512, 512), 1) // 64).astype(F32).astype(BF16)

    def unit(v):
        squares = nn((v * v).astype(BF16), same_head)
        return v * lax.rsqrt(squares * (1.0 / 64) + EPS)

    query = unit(nt(x, all4[0]))
    key = unit(nt(x, all4[1])).astype(BF16)
    value = nt(x, all4[2])
    same_sample = iota((128, 128), 0) // 64 == iota((128, 128), 1) // 64
    heads = []
    for i in range(4):
        span = slice(128 * i, 128 * i + 128)
        q, k, v = query[:, span], key[:, span], value[:, span]
        parts = []
        for s in range(2):
            half = left if s == 0 else jnp.logical_not(left)
            scores = nt(jnp.where(half, q, 0.0).astype(BF16), k) * (all_sharp[2 * i + s, 0:1, :] * (1.0 / 64))
            e = jnp.where(same_sample, jnp.exp(scores), 0.0).astype(BF16)
            o = nn(e, jnp.where(half, v, 1.0).astype(BF16))
            parts.append(o / pltpu.roll(o, 64, 1))
        heads.append(jnp.where(left, parts[0], parts[1]).astype(BF16))
    summed = nn(jnp.concatenate(heads, axis=1), all4[3]) + x.astype(F32)
    mean = jnp.mean(summed * summed, axis=1, keepdims=True)
    nall[tensor] = (summed * lax.rsqrt(mean + EPS) * gain_ref[...]).astype(BF16)

    def pass_on(rows, n, to):
        return remote(rows, rows, ass.at[n], ars.at[n], tensor=to)

    pass_on(nall.at[tensor], 0, at(1, 0)).start()
    for k in ring:
        pass_on(nall.at[tensor], k, at(0, k)).start()

    off = jnp.sum(jnp.where(iota((64, 64), 0) == iota((64, 64), 1), off_ref[...], 0.0), axis=1, keepdims=True)

    def chunk(r, carry):
        m = lax.rem(r + 1, 3)
        dy = (r + 6) // 8 * (1 + 2 * m - 3 * (m // 2))
        dh = r // 5 + (r + 7) // 8 - (r + 6) // 8
        i = at(dh, -dy)
        first, second = nall.at[i, 0:64], nall.at[i, 64:128]

        @pl.when(r == 1)
        def _():
            pass_on(nall.at[i], 0, at(1, 0)).wait_recv()
            for k in ring:
                pass_on(first, 4 + k, at(0, k)).start()

        @pl.when(jnp.logical_and(r >= 2, r <= 4))
        def _():
            pass_on(nall.at[i], dy, at(1, 0)).wait_recv()
            pass_on(second, 8 + dy, at(1, 0)).start()

        @pl.when(r >= 5)
        def _():
            pass_on(first, 4 + dy, at(1, 0)).wait_recv()
            pass_on(second, 8 + dy, at(1, 0)).wait_recv()

        n = nall[i]
        h = nt(wup_t[...], n)
        sg = 1.0 / (1.0 + jnp.exp(-h))
        act = (h * sg).astype(BF16)
        slope = (back[i] * sg * (1.0 + h * (1.0 - sg))).astype(BF16)
        mlp[i] = nn(wdn_t[...], act).astype(BF16)
        rows = cot_ref[pl.ds(pl.multiple_of(128 * i, 128), 128), :]
        down = nn(act, rows)
        up = nt(n.T, slope)
        side = nn(ctt[i].astype(BF16), n)
        for t in range(4):
            span = slice(128 * t, 128 * t + 128)
            g32[512 * t : 512 * t + 512] += up[:, span]
            g32[2048 + 512 * t : 2560 + 512 * t] += down[:, span]
            g32[4096 + 64 * t : 4160 + 64 * t] += side[:, span]
        c = nt(low[...], n)
        cross[i] = xt[i] * (c[0:64] + off) + c[64:128]
        return carry

    lax.fori_loop(0, TENSOR, chunk, 0)
    g32[4352:4416] = jnp.broadcast_to(bias, (64, 128))

    gb16[...] = g32[...].astype(BF16)

    def owned(zz):
        zz = lax.rem(zz + 2 * Z, Z)
        return pl.multiple_of(CLASS * lax.rem(zz, 4) + CHUNK * (zz // 4), 16)

    def rows_of(c, zz):
        return pl.ds(pl.multiple_of(HALF * c + owned(zz), 16), CHUNK)

    steps = (8, 4, 12, 0)
    cores = []
    for k in steps:
        for d in (1, -1, 2 - 4 * core, 0):
            n = len(cores)
            copy = remote(
                gb16.at[rows_of(1 - core, z + d + k), :], crecv.at[n], css.at[8 + n], crs.at[8 + n], table=sibling
            )
            copy.start()
            cores.append(copy)
    terms = []
    for k in range(1, TENSOR):
        to = tensor_at(k)
        rows = mlp.at[:, pl.ds(pl.multiple_of(64 * to, 64), 64), :]
        copy = remote(rows, rs.at[k - 1], mss.at[k], mrs.at[k], tensor=to)
        copy.start()
        terms.append(copy)

    near_z = (1, -1, 4 * core - 2)
    near_by = (2, -2, 8 * core - 4)
    near = []
    for s, k in enumerate(steps):
        for i in range(3):
            n = 4 * s + i
            cores[n].wait_recv()
            part = g32[rows_of(core, z + near_z[i] + k), :] + crecv[n].astype(F32)
            hb16[3 * s + i] = part.astype(BF16)
            copy = remote(hb16.at[3 * s + i], nr.at[3 * s + i], gss.at[3 * s + i], grs.at[3 * s + i], table=around(near_by[i]))
            copy.start()
            near.append(copy)
    far = []
    for s, k in enumerate(steps):
        n = 4 * s + 3
        cores[n].wait_recv()
        total = g32[rows_of(core, z + k), :] + crecv[n].astype(F32)
        for i in range(3):
            near[3 * s + i].wait_recv()
            total = total + nr[3 * s + i].astype(F32)
        if k:
            cb16[s] = total.astype(BF16)
            copy = remote(cb16.at[s], fr.at[s], gss.at[12 + s], grs.at[12 + s], table=around(2 * k))
            copy.start()
            far.append(copy)
        else:
            c32[...] = total
    for copy in far:
        copy.wait_recv()
    total = c32[...] + fr[0].astype(F32) + fr[1].astype(F32) + fr[2].astype(F32)
    fb16[...] = total.astype(BF16)
    twin = remote(fb16, dr, gss.at[15], grs.at[15], dp=1 - dp)
    twin.start()
    twin.wait_recv()
    gfin[rows_of(core, z), :] = (fb16[...].astype(F32) + dr[...].astype(F32)).astype(BF16)

    back_far, back_near, across = [], [], []

    def same(zz, s, device):
        block = gfin.at[rows_of(core, zz), :]
        copy = remote(block, block, gss.at[s], grs.at[s], table=device)
        copy.start()
        return copy

    def hand_on(zz, s):
        for i in range(3):
            back_near.append(same(zz, 19 + 3 * s + i, around(near_by[i])))
        across.append(same(zz, 31 + s, sibling))

    for s in range(3):
        back_far.append(same(z, 16 + s, around(2 * steps[s])))
    hand_on(z, 3)

    for copy in terms:
        copy.wait_recv()

    def finish(i, carry):
        own = mlp[i, pl.ds(pl.multiple_of(64 * tensor, 64), 64), :].astype(F32)
        for k in range(1, TENSOR):
            own = own + rs[k - 1, i].astype(F32)
        out = (cross[i] + own).T
        mixed_ref[2 * i] = out[0:64].astype(BF16)
        mixed_ref[2 * i + 1] = out[64:128].astype(BF16)
        return carry

    lax.fori_loop(0, TENSOR, finish, 0)
    for s in (1, 2, 0):
        back_far[s].wait_recv()
        hand_on(z - steps[s], s)
    for order, s in enumerate((3, 1, 2, 0)):
        for i in range(3):
            back_near[3 * order + i].wait_recv()
            across.append(same(z - near_z[i] - steps[s], 35 + 3 * s + i, sibling))
    for copy in across:
        copy.wait_recv()

    for copy in to_table + to_tensor + weights + sharps + over + cores + terms + near + far + [twin] + back_far + back_near + across:
        copy.wait_send()
    pass_on(nall.at[tensor], 0, at(1, 0)).wait_send()
    for k in ring:
        pass_on(nall.at[tensor], k, at(0, k)).wait_send()
        pass_on(nall.at[tensor, 0:64], 4 + k, at(0, k)).wait_send()
        pass_on(nall.at[tensor, 64:128], 8 + k, at(1, 0)).wait_send()


def write_out(mixed_ref, g_ref, mixed_hbm, gc_hbm, gb_hbm, gu_hbm, gd_hbm, gc, gb, gu, gd, sems):
    copies = []

    def send(ref, hbm):
        copies.append(pltpu.make_async_copy(ref, hbm, sems.at[len(copies)]))
        copies[-1].start()

    send(mixed_ref, mixed_hbm)
    for t in range(4):
        gu[:, 128 * t : 128 * t + 128] = g_ref[512 * t : 512 * t + 512].astype(F32)
    send(gu, gu_hbm)
    for t in range(4):
        gd[:, 128 * t : 128 * t + 128] = g_ref[2048 + 512 * t : 2560 + 512 * t].astype(F32)
    send(gd, gd_hbm)
    for t in range(4):
        gc[:, 128 * t : 128 * t + 128] = g_ref[4096 + 64 * t : 4160 + 64 * t].astype(F32)
    send(gc, gc_hbm)
    gb[...] = g_ref[4352:4416].astype(F32).T[0:1]
    send(gb, gb_hbm)
    for copy in copies:
        copy.wait()


def body(
    fetched_table_entries,
    position_category_number,
    category_shift_vector,
    asker_matcher_content_matrix,
    affinity_sharpness,
    mixer_exit_matrix,
    mixer_rescale_factor,
    interact_matrix,
    interact_offset_vector,
    widening_matrix,
    narrowing_matrix,
    incoming_cotangent,
):
    vmem = pl.BlockSpec(memory_space=pltpu.VMEM)
    operands = (
        jnp.transpose(fetched_table_entries, (0, 2, 1)).reshape(128, 512),
        position_category_number.reshape(1, 64),
        category_shift_vector,
        jnp.transpose(asker_matcher_content_matrix, (1, 2, 0)),
        affinity_sharpness.reshape(1, 1),
        mixer_exit_matrix,
        mixer_rescale_factor.reshape(1, 512),
        interact_matrix.T,
        interact_offset_vector.reshape(1, 64),
        widening_matrix,
        narrowing_matrix,
        incoming_cotangent.reshape(1024, 512),
    )
    dma = pltpu.SemaphoreType.DMA
    scratch = [
        pltpu.VMEM((128, 512), BF16),
        pltpu.VMEM((1, 64), jnp.int32),
        pltpu.VMEM((64, 64), F32),
        pltpu.VMEM((1, 512), F32),
        pltpu.VMEM((1, 64), F32),
        pltpu.VMEM((1, 1), F32),
        pltpu.VMEM((512, 512), BF16),
        pltpu.VMEM((512, 512), BF16),
        pltpu.VMEM((1024, 512), BF16),
        pltpu.VMEM((512, 128), BF16),
        pltpu.VMEM((32, 16, 128), BF16),
        pltpu.VMEM((32, 16, 128), F32),
        pltpu.VMEM((8, 64, 128), BF16),
        pltpu.VMEM((8, 64, 128), BF16),
        pltpu.VMEM((4, 64, 512), BF16),
        pltpu.VMEM((4, 512, 512), BF16),
        pltpu.VMEM((8, 128), F32),
        pltpu.VMEM((8, 8, 128), F32),
        pltpu.VMEM((128, 512), BF16),
        pltpu.VMEM((8, 128, 512), BF16),
        pltpu.VMEM((8, 512, 128), F32),
        pltpu.VMEM((512, 512), BF16),
        pltpu.VMEM((512, 512), BF16),
        pltpu.VMEM((128, 512), BF16),
        pltpu.VMEM((8, 64, 128), F32),
        pltpu.VMEM((8, 64, 128), F32),
        pltpu.VMEM((8, 512, 128), BF16),
        pltpu.VMEM((7, 8, 64, 128), BF16),
        pltpu.VMEM((8, 64, 128), F32),
        pltpu.VMEM((ROWS, 128), F32),
        pltpu.VMEM((ROWS, 128), BF16),
        pltpu.VMEM((16, CHUNK, 128), BF16),
        pltpu.VMEM((12, CHUNK, 128), BF16),
        pltpu.VMEM((12, CHUNK, 128), BF16),
        pltpu.VMEM((CHUNK, 128), F32),
        pltpu.VMEM((3, CHUNK, 128), BF16),
        pltpu.VMEM((3, CHUNK, 128), BF16),
        pltpu.VMEM((CHUNK, 128), BF16),
        pltpu.VMEM((CHUNK, 128), BF16),
    ]
    for n in (32, 8, 12, 24, 8, 12, 8, 47):
        scratch += [dma((n,)), dma((n,))]
    scratch.append(dma((12,)))
    mixed, grads = pl.pallas_call(
        kernel,
        name="layer",
        out_shape=(pltpu.VMEM((16, 64, 64), BF16), pltpu.VMEM((ROWS, 128), BF16)),
        in_specs=[pl.BlockSpec(memory_space=pltpu.HBM)] * len(operands),
        out_specs=(vmem,) * 2,
        scratch_shapes=scratch,
        compiler_params=pltpu.CompilerParams(
            collective_id=0, has_side_effects=True, vmem_limit_bytes=58 * 2**20
        ),
    )(*operands)
    hbm = pl.BlockSpec(memory_space=pltpu.HBM)
    mixed, cross, bias, up, down = pl.pallas_call(
        write_out,
        name="write_out",
        out_shape=(
            jax.ShapeDtypeStruct((16, 64, 64), BF16),
            jax.ShapeDtypeStruct((64, 512), F32),
            jax.ShapeDtypeStruct((1, 64), F32),
            jax.ShapeDtypeStruct((512, 512), F32),
            jax.ShapeDtypeStruct((512, 512), F32),
        ),
        in_specs=(vmem,) * 2,
        out_specs=(hbm,) * 5,
        scratch_shapes=[
            pltpu.VMEM((64, 512), F32),
            pltpu.VMEM((1, 64), F32),
            pltpu.VMEM((512, 512), F32),
            pltpu.VMEM((512, 512), F32),
            dma((5,)),
        ],
        compiler_params=pltpu.CompilerParams(vmem_limit_bytes=16 * 2**20),
    )(mixed, grads)
    return mixed, cross.T, bias.reshape(64), up, down


def solution(mesh):
    in_specs = (
        P("table", "dp", "tensor"),
        P(),
        P(None, "tensor"),
        P(None, None, "tensor"),
        P("tensor"),
        P("tensor", None),
        P(),
        P(None, "tensor"),
        P("tensor"),
        P(None, "tensor"),
        P("tensor", None),
        P(("dp", "table"), None, None),
    )
    out_specs = (
        P(("dp", "table"), None, "tensor"),
        P(None, "tensor"),
        P("tensor"),
        P(None, "tensor"),
        P("tensor", None),
    )
    return jax.shard_map(body, mesh=mesh, in_specs=in_specs, out_specs=out_specs, check_vma=False)
```

```python
import functools

import jax
import jax.numpy as jnp
from jax import lax
from jax.experimental import pallas as pl
from jax.experimental.pallas import tpu as pltpu
from jax.sharding import PartitionSpec as P

MESH = pl.DeviceIdType.MESH
F32, BF16 = jnp.float32, jnp.bfloat16
EPS = 1e-06

TABLE, TENSOR, Z = 32, 8, 16
PIECE = 80
CHUNK = 2 * PIECE
CLASS = 4 * CHUNK
HALF = 4 * CLASS
ROWS = 2 * HALF
FAR_FIRST = [k for d in (8, 7, 9, 6, 10, 5, 11, 4, 12, 3, 13, 2, 14, 1, 15, 0) for k in (2 * d, 2 * d + 1) if k]


def nn(a, b):
    return jnp.dot(a, b, preferred_element_type=F32)


def nt(a, b):
    return lax.dot_general(a, b, (((1,), (1,)), ((), ())), preferred_element_type=F32)


def iota(shape, dim):
    return lax.broadcasted_iota(jnp.int32, shape, dim)


def remote(src, dst, send, recv, **device):
    return pltpu.make_async_remote_copy(
        src_ref=src, dst_ref=dst, send_sem=send, recv_sem=recv, device_id=device, device_id_type=MESH
    )


def kernel(
    f_hbm, pos_hbm, shift_hbm, wqkv_hbm, sharp_hbm, mex_hbm, gain_hbm, int_hbm, off_hbm, wup_hbm, wdn_hbm, cot_hbm,
    mixed_ref, gfin,
    f_ref, pos_ref, shift_ref, gain_ref, off_ref, sharp_ref, wup_ref, wdn_ref, cot_ref,
    zs, arr, arrf, xin, xa, own4, all4, own_sharp, all_sharp, xrow, nall, back, wup_t, wdn_t, low, xt, ctt, mlp, rs, xs, xr, cross,
    g32, gs16, crecv, db16, drecv, hb16, nr, cb16, fr,
    zss, zrs, tss, trs, wss, wrs, css, crs, sss, srs, ass, ars, mss, mrs, gss, grs, dss, drs, oss, ors, los,
):
    dp = lax.axis_index("dp")
    table = lax.axis_index("table")
    tensor = lax.axis_index("tensor")
    z, core = table // 2, lax.rem(table, 2)
    hi, y = tensor // 4, lax.rem(tensor, 4)
    sibling = table + 1 - 2 * core

    def around(k):
        return lax.rem(table + TABLE + k, TABLE)

    def tensor_at(k):
        return lax.rem(tensor + k, TENSOR)

    def settle(*groups):
        for group in groups:
            for copy in group:
                copy.wait_send()

    barrier = pltpu.get_barrier_semaphore()
    for k in FAR_FIRST:
        pl.semaphore_signal(barrier, inc=1, device_id={"table": around(k)}, device_id_type=MESH)
    for k in range(1, TENSOR):
        pl.semaphore_signal(barrier, inc=1, device_id={"tensor": tensor_at(k)}, device_id_type=MESH)
    pl.semaphore_signal(barrier, inc=1, device_id={"dp": 1 - dp}, device_id_type=MESH)

    loads = []
    for hbm, ref in (
        (f_hbm, f_ref), (wqkv_hbm, own4.at[0:3]), (mex_hbm, own4.at[3]), (sharp_hbm, sharp_ref), (wup_hbm, wup_ref),
        (wdn_hbm, wdn_ref), (int_hbm, low.at[0:64]), (cot_hbm, cot_ref), (pos_hbm, pos_ref), (shift_hbm, shift_ref),
        (gain_hbm, gain_ref), (off_hbm, off_ref),
    ):
        copy = pltpu.make_async_copy(hbm, ref, los.at[len(loads)])
        copy.start()
        loads.append(copy)

    loads[0].wait()
    zs[...] = f_ref[...].T
    arr[TABLE - 1] = zs[pl.ds(pl.multiple_of(16 * table, 16), 16), :]
    for copy in loads[1:4]:
        copy.wait()
    own_sharp[...] = jnp.broadcast_to(sharp_ref[...], own_sharp.shape)

    pl.semaphore_wait(barrier, TABLE - 1 + TENSOR - 1 + 1)

    ring = (1, 3, 2)

    def at(h, k):
        return 4 * lax.rem(hi + h, 2) + lax.rem(y + 4 + k, 4)

    def shard(block, count, owner):
        return all4.at[pl.ds(2 * core + block, count), pl.ds(pl.multiple_of(64 * owner, 64), 64), :]

    all4[pl.ds(2 * core, 2), pl.ds(pl.multiple_of(64 * tensor, 64), 64), :] = own4[pl.ds(2 * core, 2)]
    all_sharp[tensor] = own_sharp[...]
    weights, sharps = [], []

    def spread(block, count, owner, n, to):
        copy = remote(shard(block, count, owner), shard(block, count, owner), wss.at[n], wrs.at[n], tensor=to)
        copy.start()
        weights.append(copy)

    spread(0, 2, tensor, 0, at(1, 0))
    for k in ring:
        spread(0, 2, tensor, k, at(0, k))

    for k in FAR_FIRST:
        rows = zs.at[pl.ds(pl.multiple_of(16 * around(k), 16), 16), :]
        remote(rows, arr.at[k - 1], zss.at[0], zrs.at[0], table=around(k)).start()
    all_rows = remote(arr.at[0 : TABLE - 1], arr.at[0 : TABLE - 1], zss.at[0], zrs.at[0], table=around(1))
    for k in range(1, TENSOR):
        copy = remote(own_sharp, all_sharp.at[tensor], sss.at[k], srs.at[k], tensor=tensor_at(k))
        copy.start()
        sharps.append(copy)

    over = []

    def hand_over(owner):
        n = len(over)
        copy = remote(shard(0, 2, owner), shard(0, 2, owner), css.at[n], crs.at[n], table=sibling)
        copy.start()
        over.append(copy)

    hand_over(tensor)

    for copy in loads[4:]:
        copy.wait()
    wup_t[...] = wup_ref[...].T
    wdn_t[...] = wdn_ref[...].T
    low[64:128] = (iota((64, 512), 1) == 64 * tensor + iota((64, 512), 0)).astype(F32).astype(BF16)

    def backward(i, carry):
        rows = cot_ref[pl.ds(pl.multiple_of(128 * i, 128), 128), :]
        back[i] = nt(wdn_ref[...], rows)
        ctt[i] = nt(low[64:128], rows)
        return carry

    lax.fori_loop(0, TENSOR, backward, 0)
    g32[...] = jnp.zeros_like(g32)

    lane = iota((1, 128), 1)
    left = lane < 64
    hot = (iota((64, 64), 0) == pos_ref[...]).astype(F32).astype(BF16)
    j = iota((64, 64), 1)
    source = 2 * lax.rem(table - lax.rem(j, 32) - 1 + TABLE, TABLE) + j // 32
    place = nn(hot, (iota((64, 64), 0) == source).astype(F32).astype(BF16)).astype(BF16)
    shift = shift_ref[...]
    shift = jnp.concatenate([shift, shift], axis=1)

    weights[0].wait_recv()
    for k in ring:
        spread(0, 1, at(1, 0), 4 + k, at(0, k))
    hand_over(at(1, 0))
    for n, k in enumerate(ring):
        weights[1 + n].wait_recv()
        spread(1, 1, at(0, -k), 8 + k, at(1, 0))
        hand_over(at(0, -k))

    all_rows.wait_recv()
    arrf[...] = arr[...].astype(F32)
    for i in range(TENSOR):
        a, b = arrf[:, 2 * i, :], arrf[:, 2 * i + 1, :]
        even = jnp.where(left, a, pltpu.roll(b, 64, 1))
        odd = jnp.where(left, pltpu.roll(a, 64, 1), b)
        rows = jnp.concatenate([even, odd], axis=0).astype(BF16)
        xin[i] = (nn(place, rows) + shift).astype(BF16)
    to_tensor = []
    for k in range(1, TENSOR):
        copy = remote(xin.at[tensor_at(k)], xa.at[tensor], tss.at[k], trs.at[k], tensor=tensor_at(k))
        copy.start()
        to_tensor.append(copy)
    xa[tensor] = xin[tensor]

    def columns(i, carry):
        t = xin[i].astype(F32).T
        xt[i] = jnp.concatenate([t[0:64], t[64:128]], axis=1)
        return carry
    lax.fori_loop(0, TENSOR, columns, 0)
    term = ctt[...] * xt[...]
    ctt[...] = term
    bias = jnp.sum(jnp.sum(term, axis=0), axis=1, keepdims=True)

    for n, k in enumerate(ring):
        weights[4 + n].wait_recv()
        weights[7 + n].wait_recv()
        hand_over(at(1, -k))
    for copy in to_tensor + sharps:
        copy.wait_recv()

    for i in range(4):
        a, b = xa[2 * i].astype(F32), xa[2 * i + 1].astype(F32)
        span = slice(128 * i, 128 * i + 128)
        xrow[0:64, span] = jnp.where(left, a, pltpu.roll(b, 64, 1)).astype(BF16)
        xrow[64:128, span] = jnp.where(left, pltpu.roll(a, 64, 1), b).astype(BF16)
    for copy in over:
        copy.wait_recv()

    x = xrow[...]
    same_head = (iota((512, 512), 0) // 64 == iota((512, 512), 1) // 64).astype(F32).astype(BF16)

    def unit(v):
        squares = nn((v * v).astype(BF16), same_head)
        return v * lax.rsqrt(squares * (1.0 / 64) + EPS)

    query = unit(nt(x, all4[0]))
    key = unit(nt(x, all4[1])).astype(BF16)
    value = nt(x, all4[2])
    same_sample = iota((128, 128), 0) // 64 == iota((128, 128), 1) // 64
    heads = []
    for i in range(4):
        span = slice(128 * i, 128 * i + 128)
        q, k, v = query[:, span], key[:, span], value[:, span]
        parts = []
        for s in range(2):
            half = left if s == 0 else jnp.logical_not(left)
            scores = nt(jnp.where(half, q, 0.0).astype(BF16), k) * (all_sharp[2 * i + s, 0:1, :] * (1.0 / 64))
            e = jnp.where(same_sample, jnp.exp(scores), 0.0).astype(BF16)
            o = nn(e, jnp.where(half, v, 1.0).astype(BF16))
            parts.append(o / pltpu.roll(o, 64, 1))
        heads.append(jnp.where(left, parts[0], parts[1]).astype(BF16))
    summed = nn(jnp.concatenate(heads, axis=1), all4[3]) + x.astype(F32)
    mean = jnp.mean(summed * summed, axis=1, keepdims=True)
    nall[tensor] = (summed * lax.rsqrt(mean + EPS) * gain_ref[...]).astype(BF16)

    def pass_on(rows, n, to):
        return remote(rows, rows, ass.at[n], ars.at[n], tensor=to)

    pass_on(nall.at[tensor], 0, at(1, 0)).start()
    for k in ring:
        pass_on(nall.at[tensor], k, at(0, k)).start()

    settle([all_rows], to_tensor, weights, sharps, over)
    off = jnp.sum(jnp.where(iota((64, 64), 0) == iota((64, 64), 1), off_ref[...], 0.0), axis=1, keepdims=True)

    def chunk(r, carry):
        m = lax.rem(r + 1, 3)
        dy = (r + 6) // 8 * (1 + 2 * m - 3 * (m // 2))
        dh = r // 5 + (r + 7) // 8 - (r + 6) // 8
        i = at(dh, -dy)
        first, second = nall.at[i, 0:64], nall.at[i, 64:128]

        @pl.when(r == 1)
        def _():
            pass_on(nall.at[i], 0, at(1, 0)).wait_recv()
            for k in ring:
                pass_on(first, 4 + k, at(0, k)).start()

        @pl.when(jnp.logical_and(r >= 2, r <= 4))
        def _():
            pass_on(nall.at[i], dy, at(1, 0)).wait_recv()
            pass_on(second, 8 + dy, at(1, 0)).start()

        @pl.when(r >= 5)
        def _():
            pass_on(first, 4 + dy, at(1, 0)).wait_recv()
            pass_on(second, 8 + dy, at(1, 0)).wait_recv()

        n = nall[i]
        h = nt(wup_t[...], n)
        sg = 1.0 / (1.0 + jnp.exp(-h))
        act = (h * sg).astype(BF16)
        slope = (back[i] * sg * (1.0 + h * (1.0 - sg))).astype(BF16)
        mlp[i] = nn(wdn_t[...], act).astype(BF16)
        rows = cot_ref[pl.ds(pl.multiple_of(128 * i, 128), 128), :]
        down = nn(act, rows)
        up = nt(n.T, slope)
        side = nn(ctt[i].astype(BF16), n)
        for t in range(4):
            span = slice(128 * t, 128 * t + 128)
            g32[512 * t : 512 * t + 512] += up[:, span]
            g32[2048 + 512 * t : 2560 + 512 * t] += down[:, span]
            g32[4096 + 64 * t : 4160 + 64 * t] += side[:, span]
        c = nt(low[...], n)
        cross[i] = xt[i] * (c[0:64] + off) + c[64:128]
        return carry

    lax.fori_loop(0, TENSOR, chunk, 0)
    g32[4352:4416] = jnp.broadcast_to(bias, (64, 128))

    def rows_of(c, zz, d, count):
        zz = lax.rem(zz + 2 * Z, Z)
        start = HALF * c + CLASS * lax.rem(zz, 4) + CHUNK * (zz // 4) + PIECE * d
        return pl.ds(pl.multiple_of(start, 16), count)

    def half(d):
        return pl.ds(pl.multiple_of(PIECE * d, 16), PIECE)

    steps = (8, 4, 12, 0)
    near_z = (1, -1, 4 * core - 2)
    near_by = (2, -2, 8 * core - 4)
    cores, twins, near, far = [], [], [], []
    for s, k in enumerate(steps):
        for j, d in enumerate((1, -1, 2 - 4 * core, 0)):
            gs16[4 * s + j] = g32[rows_of(1 - core, z + d + k, 0, CHUNK), :].astype(BF16)
        four = pl.ds(4 * s, 4)
        copy = remote(gs16.at[four], crecv.at[four], css.at[8 + s], crs.at[8 + s], table=sibling)
        copy.start()
        cores.append(copy)

    def columns_of(h, k):
        return pl.ds(pl.multiple_of(64 * at(h, k), 64), 64)

    terms = []
    for n, k in enumerate(ring):
        for h in range(2):
            copy = remote(
                mlp.at[:, columns_of(h, k), :], rs.at[2 * n + h], mss.at[2 * n + h], mrs.at[2 * n + h], tensor=at(0, k)
            )
            copy.start()
            terms.append(copy)

    for s, k in enumerate(steps):
        cores[s].wait_recv()
        for j, d in enumerate(near_z + (0,)):
            n = 4 * s + j
            theirs = g32[rows_of(core, z + d + k, 1 - dp, PIECE), :] + crecv[n, half(1 - dp), :].astype(F32)
            db16[n] = theirs.astype(BF16)
        four = pl.ds(4 * s, 4)
        copy = remote(db16.at[four], drecv.at[four], dss.at[s], drs.at[s], dp=1 - dp)
        copy.start()
        twins.append(copy)

    def ours(n, zz):
        total = g32[rows_of(core, zz, dp, PIECE), :] + crecv[n, half(dp), :].astype(F32)
        return total + drecv[n].astype(F32)

    def send_near(s):
        twins[s].wait_recv()
        for i in range(3):
            n = 3 * s + i
            hb16[n] = ours(4 * s + i, z + near_z[i] + steps[s]).astype(BF16)
            copy = remote(hb16.at[n], nr.at[n], gss.at[n], grs.at[n], table=around(near_by[i]))
            copy.start()
            near.append(copy)

    def four_chips(s):
        total = ours(4 * s + 3, z + steps[s])
        for n in range(3 * s, 3 * s + 3):
            near[n].wait_recv()
            total = total + nr[n].astype(F32)
        return total

    def send_far(s):
        cb16[s] = four_chips(s).astype(BF16)
        copy = remote(cb16.at[s], fr.at[s], gss.at[12 + s], grs.at[12 + s], table=around(2 * steps[s]))
        copy.start()
        far.append(copy)

    send_near(0)
    send_near(1)
    send_far(0)
    send_near(2)
    send_far(1)
    send_near(3)
    send_far(2)
    for copy in terms:
        copy.wait_recv()

    def term_sum(i, h):
        total = mlp[i, columns_of(h, 0), :].astype(F32)
        for n in range(3):
            total = total + rs[2 * n + h, i].astype(F32)
        return total

    def partner_terms(i, carry):
        xs[i] = term_sum(i, 1).astype(BF16)
        return carry

    lax.fori_loop(0, TENSOR, partner_terms, 0)
    terms.append(remote(xs, xr, mss.at[6], mrs.at[6], tensor=at(1, 0)))
    terms[6].start()
    total = four_chips(3)
    for n, copy in enumerate(far):
        copy.wait_recv()
        total = total + fr[n].astype(F32)
    gfin[rows_of(core, z, dp, PIECE), :] = total.astype(BF16)

    back_far, back_near, back_dp, across = {}, {}, {}, {}

    def same(zz, send, recv, n, **device):
        block = gfin.at[rows_of(core, zz, dp, PIECE), :]
        copy = remote(block, block, send.at[n], recv.at[n], **device)
        copy.start()
        return copy

    def owner(s, i):
        return z - steps[s] - (near_z + (0,))[i]

    def to_dp(s, i):
        back_dp[s, i] = same(owner(s, i), dss, drs, 16 + 4 * s + i, dp=1 - dp)

    def to_near(s):
        for i in range(3):
            back_near[s, i] = same(owner(s, 3), gss, grs, 18 + 3 * s + i, table=around(near_by[i]))

    def to_core(s, i):
        back_dp[s, i].wait_recv()
        block = gfin.at[rows_of(core, owner(s, i), 0, CHUNK), :]
        across[s, i] = remote(block, block, oss.at[4 * s + i], ors.at[4 * s + i], table=sibling)
        across[s, i].start()

    def from_near(s):
        for i in range(3):
            back_near[s, i].wait_recv()
            to_dp(s, i)

    for s in range(3):
        back_far[s] = same(z, gss, grs, 15 + s, table=around(2 * steps[s]))
    to_near(3)
    to_dp(3, 3)
    settle(cores, twins, near, far, terms[:6])
    pass_on(nall.at[tensor], 0, at(1, 0)).wait_send()
    for k in ring:
        pass_on(nall.at[tensor], k, at(0, k)).wait_send()
        pass_on(nall.at[tensor, 0:64], 4 + k, at(0, k)).wait_send()
        pass_on(nall.at[tensor, 64:128], 8 + k, at(1, 0)).wait_send()
    from_near(3)
    to_core(3, 3)
    for s in (1, 2):
        back_far[s].wait_recv()
        to_near(s)
        to_dp(s, 3)
    for i in range(3):
        to_core(3, i)
    back_far[0].wait_recv()
    to_near(0)
    to_dp(0, 3)
    from_near(1)
    from_near(2)

    terms[6].wait_recv()

    def finish(i, carry):
        own = term_sum(i, 0) + xr[i].astype(F32)
        out = (cross[i] + own).T
        mixed_ref[2 * i] = out[0:64].astype(BF16)
        mixed_ref[2 * i + 1] = out[64:128].astype(BF16)
        return carry

    lax.fori_loop(0, TENSOR, finish, 0)
    from_near(0)
    for s in (1, 2):
        for i in (3, 0, 1, 2):
            to_core(s, i)
    for i in (3, 0, 1, 2):
        to_core(0, i)
    settle(terms[6:], back_far.values(), back_near.values(), back_dp.values())
    for copy in across.values():
        copy.wait_recv()
    settle(across.values())


def write_out(mixed_ref, g_ref, mixed_hbm, gc_hbm, gb_hbm, gu_hbm, gd_hbm, gc, gb, gu, gd, sems):
    copies = []

    def send(ref, hbm):
        copies.append(pltpu.make_async_copy(ref, hbm, sems.at[len(copies)]))
        copies[-1].start()

    send(mixed_ref, mixed_hbm)
    for t in range(4):
        gu[:, 128 * t : 128 * t + 128] = g_ref[512 * t : 512 * t + 512].astype(F32)
    send(gu, gu_hbm)
    for t in range(4):
        gd[:, 128 * t : 128 * t + 128] = g_ref[2048 + 512 * t : 2560 + 512 * t].astype(F32)
    send(gd, gd_hbm)
    for t in range(4):
        gc[:, 128 * t : 128 * t + 128] = g_ref[4096 + 64 * t : 4160 + 64 * t].astype(F32)
    send(gc, gc_hbm)
    gb[...] = g_ref[4352:4416].astype(F32).T[0:1]
    send(gb, gb_hbm)
    for copy in copies:
        copy.wait()


def body(
    fetched_table_entries,
    position_category_number,
    category_shift_vector,
    asker_matcher_content_matrix,
    affinity_sharpness,
    mixer_exit_matrix,
    mixer_rescale_factor,
    interact_matrix,
    interact_offset_vector,
    widening_matrix,
    narrowing_matrix,
    incoming_cotangent,
):
    vmem = pl.BlockSpec(memory_space=pltpu.VMEM)
    operands = (
        jnp.transpose(fetched_table_entries, (0, 2, 1)).reshape(128, 512),
        position_category_number.reshape(1, 64),
        category_shift_vector,
        jnp.transpose(asker_matcher_content_matrix, (1, 2, 0)),
        affinity_sharpness.reshape(1, 1),
        mixer_exit_matrix,
        mixer_rescale_factor.reshape(1, 512),
        interact_matrix.T,
        interact_offset_vector.reshape(1, 64),
        widening_matrix,
        narrowing_matrix,
        incoming_cotangent.reshape(1024, 512),
    )
    dma = pltpu.SemaphoreType.DMA
    scratch = [
        pltpu.VMEM((128, 512), BF16),
        pltpu.VMEM((1, 64), jnp.int32),
        pltpu.VMEM((64, 64), F32),
        pltpu.VMEM((1, 512), F32),
        pltpu.VMEM((1, 64), F32),
        pltpu.VMEM((1, 1), F32),
        pltpu.VMEM((512, 512), BF16),
        pltpu.VMEM((512, 512), BF16),
        pltpu.VMEM((1024, 512), BF16),
        pltpu.VMEM((512, 128), BF16),
        pltpu.VMEM((32, 16, 128), BF16),
        pltpu.VMEM((32, 16, 128), F32),
        pltpu.VMEM((8, 64, 128), BF16),
        pltpu.VMEM((8, 64, 128), BF16),
        pltpu.VMEM((4, 64, 512), BF16),
        pltpu.VMEM((4, 512, 512), BF16),
        pltpu.VMEM((8, 128), F32),
        pltpu.VMEM((8, 8, 128), F32),
        pltpu.VMEM((128, 512), BF16),
        pltpu.VMEM((8, 128, 512), BF16),
        pltpu.VMEM((8, 512, 128), F32),
        pltpu.VMEM((512, 512), BF16),
        pltpu.VMEM((512, 512), BF16),
        pltpu.VMEM((128, 512), BF16),
        pltpu.VMEM((8, 64, 128), F32),
        pltpu.VMEM((8, 64, 128), F32),
        pltpu.VMEM((8, 512, 128), BF16),
        pltpu.VMEM((6, 8, 64, 128), BF16),
        pltpu.VMEM((8, 64, 128), BF16),
        pltpu.VMEM((8, 64, 128), BF16),
        pltpu.VMEM((8, 64, 128), F32),
        pltpu.VMEM((ROWS, 128), F32),
        pltpu.VMEM((16, CHUNK, 128), BF16),
        pltpu.VMEM((16, CHUNK, 128), BF16),
        pltpu.VMEM((16, PIECE, 128), BF16),
        pltpu.VMEM((16, PIECE, 128), BF16),
        pltpu.VMEM((12, PIECE, 128), BF16),
        pltpu.VMEM((12, PIECE, 128), BF16),
        pltpu.VMEM((3, PIECE, 128), BF16),
        pltpu.VMEM((3, PIECE, 128), BF16),
    ]
    for n in (1, 8, 12, 12, 8, 12, 7, 30, 32, 16):
        scratch += [dma((n,)), dma((n,))]
    scratch.append(dma((12,)))
    mixed, grads = pl.pallas_call(
        kernel,
        name="layer",
        out_shape=(pltpu.VMEM((16, 64, 64), BF16), pltpu.VMEM((ROWS, 128), BF16)),
        in_specs=[pl.BlockSpec(memory_space=pltpu.HBM)] * len(operands),
        out_specs=(vmem,) * 2,
        scratch_shapes=scratch,
        compiler_params=pltpu.CompilerParams(
            collective_id=0, has_side_effects=True, vmem_limit_bytes=58 * 2**20
        ),
    )(*operands)
    hbm = pl.BlockSpec(memory_space=pltpu.HBM)
    mixed, cross, bias, up, down = pl.pallas_call(
        write_out,
        name="write_out",
        out_shape=(
            jax.ShapeDtypeStruct((16, 64, 64), BF16),
            jax.ShapeDtypeStruct((64, 512), F32),
            jax.ShapeDtypeStruct((1, 64), F32),
            jax.ShapeDtypeStruct((512, 512), F32),
            jax.ShapeDtypeStruct((512, 512), F32),
        ),
        in_specs=(vmem,) * 2,
        out_specs=(hbm,) * 5,
        scratch_shapes=[
            pltpu.VMEM((64, 512), F32),
            pltpu.VMEM((1, 64), F32),
            pltpu.VMEM((512, 512), F32),
            pltpu.VMEM((512, 512), F32),
            dma((5,)),
        ],
        compiler_params=pltpu.CompilerParams(vmem_limit_bytes=16 * 2**20),
    )(mixed, grads)
    return mixed, cross.T, bias.reshape(64), up, down


def solution(mesh):
    in_specs = (
        P("table", "dp", "tensor"),
        P(),
        P(None, "tensor"),
        P(None, None, "tensor"),
        P("tensor"),
        P("tensor", None),
        P(),
        P(None, "tensor"),
        P("tensor"),
        P(None, "tensor"),
        P("tensor", None),
        P(("dp", "table"), None, None),
    )
    out_specs = (
        P(("dp", "table"), None, "tensor"),
        P(None, "tensor"),
        P("tensor"),
        P(None, "tensor"),
        P("tensor", None),
    )
    return jax.shard_map(body, mesh=mesh, in_specs=in_specs, out_specs=out_specs, check_vma=False)
```

```python
import functools

import jax
import jax.numpy as jnp
from jax import lax
from jax.experimental import pallas as pl
from jax.experimental.pallas import tpu as pltpu
from jax.sharding import PartitionSpec as P

MESH = pl.DeviceIdType.MESH
F32, BF16 = jnp.float32, jnp.bfloat16
EPS = 1e-06

TABLE, TENSOR, Z = 32, 8, 16
PIECE = 80
CHUNK = 2 * PIECE
CLASS = 4 * CHUNK
HALF = 4 * CLASS
ROWS = 2 * HALF
FAR_FIRST = [k for d in (8, 7, 9, 6, 10, 5, 11, 4, 12, 3, 13, 2, 14, 1, 15, 0) for k in (2 * d, 2 * d + 1) if k]


def nn(a, b):
    return jnp.dot(a, b, preferred_element_type=F32)


def nt(a, b):
    return lax.dot_general(a, b, (((1,), (1,)), ((), ())), preferred_element_type=F32)


def iota(shape, dim):
    return lax.broadcasted_iota(jnp.int32, shape, dim)


def remote(src, dst, send, recv, **device):
    return pltpu.make_async_remote_copy(
        src_ref=src, dst_ref=dst, send_sem=send, recv_sem=recv, device_id=device, device_id_type=MESH
    )


def kernel(
    f_hbm, pos_hbm, shift_hbm, wqkv_hbm, sharp_hbm, mex_hbm, gain_hbm, int_hbm, off_hbm, wup_hbm, wdn_hbm, cot_hbm,
    mixed_ref, gfin,
    f_ref, pos_ref, shift_ref, gain_ref, off_ref, sharp_ref, wup_ref, wdn_ref, cot_ref,
    zs, arr, arrf, xin, xa, own4, all4, own_sharp, all_sharp, xrow, nall, back, wup_t, wdn_t, low, xt, ctt, mlp, rs, xs, xr, cross,
    g32, gs16, crecv, db16, drecv, hb16, nr, cb16, fr,
    zss, zrs, tss, trs, wss, wrs, css, crs, sss, srs, ass, ars, mss, mrs, gss, grs, dss, drs, oss, ors, los,
):
    dp = lax.axis_index("dp")
    table = lax.axis_index("table")
    tensor = lax.axis_index("tensor")
    z, core = table // 2, lax.rem(table, 2)
    hi, y = tensor // 4, lax.rem(tensor, 4)
    sibling = table + 1 - 2 * core

    def around(k):
        return lax.rem(table + TABLE + k, TABLE)

    def tensor_at(k):
        return lax.rem(tensor + k, TENSOR)

    def settle(*groups):
        for group in groups:
            for copy in group:
                copy.wait_send()

    barrier = pltpu.get_barrier_semaphore()
    for k in FAR_FIRST:
        pl.semaphore_signal(barrier, inc=1, device_id={"table": around(k)}, device_id_type=MESH)
    for k in range(1, TENSOR):
        pl.semaphore_signal(barrier, inc=1, device_id={"tensor": tensor_at(k)}, device_id_type=MESH)
    pl.semaphore_signal(barrier, inc=1, device_id={"dp": 1 - dp}, device_id_type=MESH)

    loads = []
    for hbm, ref in (
        (f_hbm, f_ref), (wqkv_hbm, own4.at[0:3]), (mex_hbm, own4.at[3]), (sharp_hbm, sharp_ref), (wup_hbm, wup_ref),
        (wdn_hbm, wdn_ref), (int_hbm, low.at[0:64]), (cot_hbm, cot_ref), (pos_hbm, pos_ref), (shift_hbm, shift_ref),
        (gain_hbm, gain_ref), (off_hbm, off_ref),
    ):
        copy = pltpu.make_async_copy(hbm, ref, los.at[len(loads)])
        copy.start()
        loads.append(copy)

    loads[0].wait()
    zs[...] = f_ref[...].T
    arr[TABLE - 1] = zs[pl.ds(pl.multiple_of(16 * table, 16), 16), :]
    for copy in loads[1:4]:
        copy.wait()
    own_sharp[...] = jnp.broadcast_to(sharp_ref[...], own_sharp.shape)

    pl.semaphore_wait(barrier, TABLE - 1 + TENSOR - 1 + 1)

    ring = (1, 3, 2)

    def at(h, k):
        return 4 * lax.rem(hi + h, 2) + lax.rem(y + 4 + k, 4)

    def shard(block, count, owner):
        return all4.at[pl.ds(2 * core + block, count), pl.ds(pl.multiple_of(64 * owner, 64), 64), :]

    all4[pl.ds(2 * core, 2), pl.ds(pl.multiple_of(64 * tensor, 64), 64), :] = own4[pl.ds(2 * core, 2)]
    all_sharp[tensor] = own_sharp[...]
    weights, sharps = [], []

    def spread(block, count, owner, n, to):
        copy = remote(shard(block, count, owner), shard(block, count, owner), wss.at[n], wrs.at[n], tensor=to)
        copy.start()
        weights.append(copy)

    spread(0, 2, tensor, 0, at(1, 0))
    for k in ring:
        spread(0, 2, tensor, k, at(0, k))

    for k in FAR_FIRST:
        rows = zs.at[pl.ds(pl.multiple_of(16 * around(k), 16), 16), :]
        remote(rows, arr.at[k - 1], zss.at[0], zrs.at[0], table=around(k)).start()
    all_rows = remote(arr.at[0 : TABLE - 1], arr.at[0 : TABLE - 1], zss.at[0], zrs.at[0], table=around(1))
    for k in range(1, TENSOR):
        copy = remote(own_sharp, all_sharp.at[tensor], sss.at[k], srs.at[k], tensor=tensor_at(k))
        copy.start()
        sharps.append(copy)

    over = []

    def hand_over(owner):
        n = len(over)
        copy = remote(shard(0, 2, owner), shard(0, 2, owner), css.at[n], crs.at[n], table=sibling)
        copy.start()
        over.append(copy)

    hand_over(tensor)

    for copy in loads[4:]:
        copy.wait()
    wup_t[...] = wup_ref[...].T
    wdn_t[...] = wdn_ref[...].T
    low[64:128] = (iota((64, 512), 1) == 64 * tensor + iota((64, 512), 0)).astype(F32).astype(BF16)

    def backward(i, carry):
        rows = cot_ref[pl.ds(pl.multiple_of(128 * i, 128), 128), :]
        back[i] = nt(wdn_ref[...], rows)
        ctt[i] = nt(low[64:128], rows)
        return carry

    lax.fori_loop(0, TENSOR, backward, 0)
    g32[...] = jnp.zeros_like(g32)

    lane = iota((1, 128), 1)
    left = lane < 64
    hot = (iota((64, 64), 0) == pos_ref[...]).astype(F32).astype(BF16)
    j = iota((64, 64), 1)
    source = 2 * lax.rem(table - lax.rem(j, 32) - 1 + TABLE, TABLE) + j // 32
    place = nn(hot, (iota((64, 64), 0) == source).astype(F32).astype(BF16)).astype(BF16)
    shift = shift_ref[...]
    shift = jnp.concatenate([shift, shift], axis=1)

    weights[0].wait_recv()
    for k in ring:
        spread(0, 1, at(1, 0), 4 + k, at(0, k))
    hand_over(at(1, 0))
    for n, k in enumerate(ring):
        weights[1 + n].wait_recv()
        spread(1, 1, at(0, -k), 8 + k, at(1, 0))
        hand_over(at(0, -k))

    all_rows.wait_recv()
    arrf[...] = arr[...].astype(F32)
    for i in range(TENSOR):
        a, b = arrf[:, 2 * i, :], arrf[:, 2 * i + 1, :]
        even = jnp.where(left, a, pltpu.roll(b, 64, 1))
        odd = jnp.where(left, pltpu.roll(a, 64, 1), b)
        rows = jnp.concatenate([even, odd], axis=0).astype(BF16)
        xin[i] = (nn(place, rows) + shift).astype(BF16)
    to_tensor = []
    for k in range(1, TENSOR):
        copy = remote(xin.at[tensor_at(k)], xa.at[tensor], tss.at[k], trs.at[k], tensor=tensor_at(k))
        copy.start()
        to_tensor.append(copy)
    xa[tensor] = xin[tensor]

    def columns(i, carry):
        t = xin[i].astype(F32).T
        xt[i] = jnp.concatenate([t[0:64], t[64:128]], axis=1)
        return carry
    lax.fori_loop(0, TENSOR, columns, 0)
    term = ctt[...] * xt[...]
    ctt[...] = term
    bias = jnp.sum(jnp.sum(term, axis=0), axis=1, keepdims=True)

    for n, k in enumerate(ring):
        weights[4 + n].wait_recv()
        weights[7 + n].wait_recv()
        hand_over(at(1, -k))
    for copy in to_tensor + sharps:
        copy.wait_recv()

    for i in range(4):
        a, b = xa[2 * i].astype(F32), xa[2 * i + 1].astype(F32)
        span = slice(128 * i, 128 * i + 128)
        xrow[0:64, span] = jnp.where(left, a, pltpu.roll(b, 64, 1)).astype(BF16)
        xrow[64:128, span] = jnp.where(left, pltpu.roll(a, 64, 1), b).astype(BF16)
    for copy in over:
        copy.wait_recv()

    x = xrow[...]
    spans = [slice(128 * i, 128 * i + 128) for i in range(4)]
    same = iota((128, 128), 0) // 64 == iota((128, 128), 1) // 64
    same_head = same.astype(F32).astype(BF16)
    query, key, value = nt(x, all4[0]), nt(x, all4[1]), nt(x, all4[2])
    pairs = jnp.concatenate([query[:, span] for span in spans] + [key[:, span] for span in spans], axis=0)
    pairs = pairs * lax.rsqrt(nn((pairs * pairs).astype(BF16), same_head) * (1.0 / 64) + EPS)
    ones = jnp.concatenate([jnp.where(left, 1.0, jnp.zeros((128, 128), F32)), jnp.where(left, jnp.zeros((128, 128), F32), 1.0)], axis=0)
    heads = []
    for i in range(4):
        q, k = pairs[128 * i : 128 * i + 128], pairs[512 + 128 * i : 640 + 128 * i].astype(BF16)
        both = jnp.concatenate([jnp.where(left, q, 0.0), jnp.where(left, 0.0, q)], axis=0).astype(BF16)
        scores = nt(both, k)
        e = [
            jnp.where(same, jnp.exp(scores[128 * s : 128 * s + 128] * (all_sharp[2 * i + s, 0:1, :] * (1.0 / 64))), 0.0)
            for s in range(2)
        ]
        v = value[:, spans[i]]
        v = jnp.concatenate([jnp.where(left, v, 0.0), jnp.where(left, 0.0, v)], axis=0)
        v = jnp.concatenate([v, ones], axis=1).astype(BF16)
        o = nn(jnp.concatenate(e, axis=1).astype(BF16), v)
        heads.append((o[:, 0:128] / o[:, 128:256]).astype(BF16))
    summed = nn(jnp.concatenate(heads, axis=1), all4[3]) + x.astype(F32)
    mean = jnp.mean(summed * summed, axis=1, keepdims=True)
    nall[tensor] = (summed * lax.rsqrt(mean + EPS) * gain_ref[...]).astype(BF16)

    def pass_on(rows, n, to):
        return remote(rows, rows, ass.at[n], ars.at[n], tensor=to)

    pass_on(nall.at[tensor], 0, at(1, 0)).start()
    for k in ring:
        pass_on(nall.at[tensor], k, at(0, k)).start()

    settle([all_rows], to_tensor, weights, sharps, over)
    off = jnp.sum(jnp.where(iota((64, 64), 0) == iota((64, 64), 1), off_ref[...], 0.0), axis=1, keepdims=True)

    def chunk(r, carry):
        m = lax.rem(r + 1, 3)
        dy = (r + 6) // 8 * (1 + 2 * m - 3 * (m // 2))
        dh = r // 5 + (r + 7) // 8 - (r + 6) // 8
        i = at(dh, -dy)
        first, second = nall.at[i, 0:64], nall.at[i, 64:128]

        @pl.when(r == 1)
        def _():
            pass_on(nall.at[i], 0, at(1, 0)).wait_recv()
            for k in ring:
                pass_on(first, 4 + k, at(0, k)).start()

        @pl.when(jnp.logical_and(r >= 2, r <= 4))
        def _():
            pass_on(nall.at[i], dy, at(1, 0)).wait_recv()
            pass_on(second, 8 + dy, at(1, 0)).start()

        @pl.when(r >= 5)
        def _():
            pass_on(first, 4 + dy, at(1, 0)).wait_recv()
            pass_on(second, 8 + dy, at(1, 0)).wait_recv()

        n = nall[i]
        h = nt(wup_t[...], n)
        sg = 1.0 / (1.0 + jnp.exp(-h))
        act = (h * sg).astype(BF16)
        slope = (back[i] * sg * (1.0 + h * (1.0 - sg))).astype(BF16)
        mlp[i] = nn(wdn_t[...], act).astype(BF16)
        rows = cot_ref[pl.ds(pl.multiple_of(128 * i, 128), 128), :]
        down = nn(act, rows)
        up = nt(n.T, slope)
        side = nn(ctt[i].astype(BF16), n)
        for t in range(4):
            span = slice(128 * t, 128 * t + 128)
            g32[512 * t : 512 * t + 512] += up[:, span]
            g32[2048 + 512 * t : 2560 + 512 * t] += down[:, span]
            g32[4096 + 64 * t : 4160 + 64 * t] += side[:, span]
        c = nt(low[...], n)
        cross[i] = xt[i] * (c[0:64] + off) + c[64:128]
        return carry

    lax.fori_loop(0, TENSOR, chunk, 0)
    g32[4352:4416] = jnp.broadcast_to(bias, (64, 128))

    def rows_of(c, zz, d, count):
        zz = lax.rem(zz + 2 * Z, Z)
        start = HALF * c + CLASS * lax.rem(zz, 4) + CHUNK * (zz // 4) + PIECE * d
        return pl.ds(pl.multiple_of(start, 16), count)

    def half(d):
        return pl.ds(pl.multiple_of(PIECE * d, 16), PIECE)

    steps = (8, 4, 12, 0)
    near_z = (1, -1, 4 * core - 2)
    near_by = (2, -2, 8 * core - 4)
    cores, twins, near, far = [], [], [], []
    for s, k in enumerate(steps):
        for j, d in enumerate((1, -1, 2 - 4 * core, 0)):
            gs16[4 * s + j] = g32[rows_of(1 - core, z + d + k, 0, CHUNK), :].astype(BF16)
        four = pl.ds(4 * s, 4)
        copy = remote(gs16.at[four], crecv.at[four], css.at[8 + s], crs.at[8 + s], table=sibling)
        copy.start()
        cores.append(copy)

    def columns_of(h, k):
        return pl.ds(pl.multiple_of(64 * at(h, k), 64), 64)

    terms = []
    for n, k in enumerate(ring):
        for h in range(2):
            copy = remote(
                mlp.at[:, columns_of(h, k), :], rs.at[2 * n + h], mss.at[2 * n + h], mrs.at[2 * n + h], tensor=at(0, k)
            )
            copy.start()
            terms.append(copy)

    for s, k in enumerate(steps):
        cores[s].wait_recv()
        for j, d in enumerate(near_z + (0,)):
            n = 4 * s + j
            theirs = g32[rows_of(core, z + d + k, 1 - dp, PIECE), :] + crecv[n, half(1 - dp), :].astype(F32)
            db16[n] = theirs.astype(BF16)
        four = pl.ds(4 * s, 4)
        copy = remote(db16.at[four], drecv.at[four], dss.at[s], drs.at[s], dp=1 - dp)
        copy.start()
        twins.append(copy)

    def ours(n, zz):
        total = g32[rows_of(core, zz, dp, PIECE), :] + crecv[n, half(dp), :].astype(F32)
        return total + drecv[n].astype(F32)

    def send_near(s):
        twins[s].wait_recv()
        for i in range(3):
            n = 3 * s + i
            hb16[n] = ours(4 * s + i, z + near_z[i] + steps[s]).astype(BF16)
            copy = remote(hb16.at[n], nr.at[n], gss.at[n], grs.at[n], table=around(near_by[i]))
            copy.start()
            near.append(copy)

    def four_chips(s):
        total = ours(4 * s + 3, z + steps[s])
        for n in range(3 * s, 3 * s + 3):
            near[n].wait_recv()
            total = total + nr[n].astype(F32)
        return total

    def send_far(s):
        cb16[s] = four_chips(s).astype(BF16)
        copy = remote(cb16.at[s], fr.at[s], gss.at[12 + s], grs.at[12 + s], table=around(2 * steps[s]))
        copy.start()
        far.append(copy)

    send_near(0)
    send_near(1)
    send_far(0)
    send_near(2)
    send_far(1)
    send_near(3)
    send_far(2)
    for copy in terms:
        copy.wait_recv()

    def term_sum(i, h):
        total = mlp[i, columns_of(h, 0), :].astype(F32)
        for n in range(3):
            total = total + rs[2 * n + h, i].astype(F32)
        return total

    def partner_terms(i, carry):
        xs[i] = term_sum(i, 1).astype(BF16)
        return carry

    lax.fori_loop(0, TENSOR, partner_terms, 0)
    terms.append(remote(xs, xr, mss.at[6], mrs.at[6], tensor=at(1, 0)))
    terms[6].start()
    total = four_chips(3)
    for n, copy in enumerate(far):
        copy.wait_recv()
        total = total + fr[n].astype(F32)
    gfin[rows_of(core, z, dp, PIECE), :] = total.astype(BF16)

    back_far, back_near, back_dp, across = {}, {}, {}, {}

    def send_same(zz, send, recv, n, **device):
        block = gfin.at[rows_of(core, zz, dp, PIECE), :]
        copy = remote(block, block, send.at[n], recv.at[n], **device)
        copy.start()
        return copy

    def owner(s, i):
        return z - steps[s] - (near_z + (0,))[i]

    def to_dp(s, i):
        back_dp[s, i] = send_same(owner(s, i), dss, drs, 16 + 4 * s + i, dp=1 - dp)

    def to_near(s):
        for i in range(3):
            back_near[s, i] = send_same(owner(s, 3), gss, grs, 18 + 3 * s + i, table=around(near_by[i]))

    def to_core(s, i):
        back_dp[s, i].wait_recv()
        block = gfin.at[rows_of(core, owner(s, i), 0, CHUNK), :]
        across[s, i] = remote(block, block, oss.at[4 * s + i], ors.at[4 * s + i], table=sibling)
        across[s, i].start()

    def from_near(s):
        for i in range(3):
            back_near[s, i].wait_recv()
            to_dp(s, i)

    for s in range(3):
        back_far[s] = send_same(z, gss, grs, 15 + s, table=around(2 * steps[s]))
    to_near(3)
    to_dp(3, 3)
    settle(cores, twins, near, far, terms[:6])
    pass_on(nall.at[tensor], 0, at(1, 0)).wait_send()
    for k in ring:
        pass_on(nall.at[tensor], k, at(0, k)).wait_send()
        pass_on(nall.at[tensor, 0:64], 4 + k, at(0, k)).wait_send()
        pass_on(nall.at[tensor, 64:128], 8 + k, at(1, 0)).wait_send()
    from_near(3)
    to_core(3, 3)
    for s in (1, 2):
        back_far[s].wait_recv()
        to_near(s)
        to_dp(s, 3)
    for i in range(3):
        to_core(3, i)
    back_far[0].wait_recv()
    to_near(0)
    to_dp(0, 3)
    from_near(1)
    from_near(2)

    terms[6].wait_recv()

    def finish(i, carry):
        own = term_sum(i, 0) + xr[i].astype(F32)
        out = (cross[i] + own).T
        mixed_ref[2 * i] = out[0:64].astype(BF16)
        mixed_ref[2 * i + 1] = out[64:128].astype(BF16)
        return carry

    lax.fori_loop(0, TENSOR, finish, 0)
    from_near(0)
    for s in (1, 2):
        for i in (3, 0, 1, 2):
            to_core(s, i)
    for i in (3, 0, 1, 2):
        to_core(0, i)
    settle(terms[6:], back_far.values(), back_near.values(), back_dp.values())
    for copy in across.values():
        copy.wait_recv()
    settle(across.values())


def write_out(mixed_ref, g_ref, mixed_hbm, gc_hbm, gb_hbm, gu_hbm, gd_hbm, gc, gb, gu, gd, sems):
    copies = []

    def send(ref, hbm):
        copies.append(pltpu.make_async_copy(ref, hbm, sems.at[len(copies)]))
        copies[-1].start()

    send(mixed_ref, mixed_hbm)
    for t in range(4):
        gu[:, 128 * t : 128 * t + 128] = g_ref[512 * t : 512 * t + 512].astype(F32)
    send(gu, gu_hbm)
    for t in range(4):
        gd[:, 128 * t : 128 * t + 128] = g_ref[2048 + 512 * t : 2560 + 512 * t].astype(F32)
    send(gd, gd_hbm)
    for t in range(4):
        gc[:, 128 * t : 128 * t + 128] = g_ref[4096 + 64 * t : 4160 + 64 * t].astype(F32)
    send(gc, gc_hbm)
    gb[...] = g_ref[4352:4416].astype(F32).T[0:1]
    send(gb, gb_hbm)
    for copy in copies:
        copy.wait()


def body(
    fetched_table_entries,
    position_category_number,
    category_shift_vector,
    asker_matcher_content_matrix,
    affinity_sharpness,
    mixer_exit_matrix,
    mixer_rescale_factor,
    interact_matrix,
    interact_offset_vector,
    widening_matrix,
    narrowing_matrix,
    incoming_cotangent,
):
    vmem = pl.BlockSpec(memory_space=pltpu.VMEM)
    operands = (
        jnp.transpose(fetched_table_entries, (0, 2, 1)).reshape(128, 512),
        position_category_number.reshape(1, 64),
        category_shift_vector,
        jnp.transpose(asker_matcher_content_matrix, (1, 2, 0)),
        affinity_sharpness.reshape(1, 1),
        mixer_exit_matrix,
        mixer_rescale_factor.reshape(1, 512),
        interact_matrix.T,
        interact_offset_vector.reshape(1, 64),
        widening_matrix,
        narrowing_matrix,
        incoming_cotangent.reshape(1024, 512),
    )
    dma = pltpu.SemaphoreType.DMA
    scratch = [
        pltpu.VMEM((128, 512), BF16),
        pltpu.VMEM((1, 64), jnp.int32),
        pltpu.VMEM((64, 64), F32),
        pltpu.VMEM((1, 512), F32),
        pltpu.VMEM((1, 64), F32),
        pltpu.VMEM((1, 1), F32),
        pltpu.VMEM((512, 512), BF16),
        pltpu.VMEM((512, 512), BF16),
        pltpu.VMEM((1024, 512), BF16),
        pltpu.VMEM((512, 128), BF16),
        pltpu.VMEM((32, 16, 128), BF16),
        pltpu.VMEM((32, 16, 128), F32),
        pltpu.VMEM((8, 64, 128), BF16),
        pltpu.VMEM((8, 64, 128), BF16),
        pltpu.VMEM((4, 64, 512), BF16),
        pltpu.VMEM((4, 512, 512), BF16),
        pltpu.VMEM((8, 128), F32),
        pltpu.VMEM((8, 8, 128), F32),
        pltpu.VMEM((128, 512), BF16),
        pltpu.VMEM((8, 128, 512), BF16),
        pltpu.VMEM((8, 512, 128), F32),
        pltpu.VMEM((512, 512), BF16),
        pltpu.VMEM((512, 512), BF16),
        pltpu.VMEM((128, 512), BF16),
        pltpu.VMEM((8, 64, 128), F32),
        pltpu.VMEM((8, 64, 128), F32),
        pltpu.VMEM((8, 512, 128), BF16),
        pltpu.VMEM((6, 8, 64, 128), BF16),
        pltpu.VMEM((8, 64, 128), BF16),
        pltpu.VMEM((8, 64, 128), BF16),
        pltpu.VMEM((8, 64, 128), F32),
        pltpu.VMEM((ROWS, 128), F32),
        pltpu.VMEM((16, CHUNK, 128), BF16),
        pltpu.VMEM((16, CHUNK, 128), BF16),
        pltpu.VMEM((16, PIECE, 128), BF16),
        pltpu.VMEM((16, PIECE, 128), BF16),
        pltpu.VMEM((12, PIECE, 128), BF16),
        pltpu.VMEM((12, PIECE, 128), BF16),
        pltpu.VMEM((3, PIECE, 128), BF16),
        pltpu.VMEM((3, PIECE, 128), BF16),
    ]
    for n in (1, 8, 12, 12, 8, 12, 7, 30, 32, 16):
        scratch += [dma((n,)), dma((n,))]
    scratch.append(dma((12,)))
    mixed, grads = pl.pallas_call(
        kernel,
        name="layer",
        out_shape=(pltpu.VMEM((16, 64, 64), BF16), pltpu.VMEM((ROWS, 128), BF16)),
        in_specs=[pl.BlockSpec(memory_space=pltpu.HBM)] * len(operands),
        out_specs=(vmem,) * 2,
        scratch_shapes=scratch,
        compiler_params=pltpu.CompilerParams(
            collective_id=0, has_side_effects=True, vmem_limit_bytes=58 * 2**20
        ),
    )(*operands)
    hbm = pl.BlockSpec(memory_space=pltpu.HBM)
    mixed, cross, bias, up, down = pl.pallas_call(
        write_out,
        name="write_out",
        out_shape=(
            jax.ShapeDtypeStruct((16, 64, 64), BF16),
            jax.ShapeDtypeStruct((64, 512), F32),
            jax.ShapeDtypeStruct((1, 64), F32),
            jax.ShapeDtypeStruct((512, 512), F32),
            jax.ShapeDtypeStruct((512, 512), F32),
        ),
        in_specs=(vmem,) * 2,
        out_specs=(hbm,) * 5,
        scratch_shapes=[
            pltpu.VMEM((64, 512), F32),
            pltpu.VMEM((1, 64), F32),
            pltpu.VMEM((512, 512), F32),
            pltpu.VMEM((512, 512), F32),
            dma((5,)),
        ],
        compiler_params=pltpu.CompilerParams(vmem_limit_bytes=16 * 2**20),
    )(mixed, grads)
    return mixed, cross.T, bias.reshape(64), up, down


def solution(mesh):
    in_specs = (
        P("table", "dp", "tensor"),
        P(),
        P(None, "tensor"),
        P(None, None, "tensor"),
        P("tensor"),
        P("tensor", None),
        P(),
        P(None, "tensor"),
        P("tensor"),
        P(None, "tensor"),
        P("tensor", None),
        P(("dp", "table"), None, None),
    )
    out_specs = (
        P(("dp", "table"), None, "tensor"),
        P(None, "tensor"),
        P("tensor"),
        P(None, "tensor"),
        P("tensor", None),
    )
    return jax.shard_map(body, mesh=mesh, in_specs=in_specs, out_specs=out_specs, check_vma=False)
```

```python
import functools

import jax
import jax.numpy as jnp
from jax import lax
from jax.experimental import pallas as pl
from jax.experimental.pallas import tpu as pltpu
from jax.sharding import PartitionSpec as P

MESH = pl.DeviceIdType.MESH
F32, BF16 = jnp.float32, jnp.bfloat16
EPS = 1e-06

TABLE, TENSOR, Z = 32, 8, 16
PIECE = 80
CHUNK = 2 * PIECE
CLASS = 4 * CHUNK
HALF = 4 * CLASS
ROWS = 2 * HALF
FAR_FIRST = [k for d in (8, 7, 9, 6, 10, 5, 11, 4, 12, 3, 13, 2, 14, 1, 15, 0) for k in (2 * d, 2 * d + 1) if k]


def nn(a, b):
    return jnp.dot(a, b, preferred_element_type=F32)


def nt(a, b):
    return lax.dot_general(a, b, (((1,), (1,)), ((), ())), preferred_element_type=F32)


def iota(shape, dim):
    return lax.broadcasted_iota(jnp.int32, shape, dim)


def remote(src, dst, send, recv, **device):
    return pltpu.make_async_remote_copy(
        src_ref=src, dst_ref=dst, send_sem=send, recv_sem=recv, device_id=device, device_id_type=MESH
    )


def kernel(
    f_hbm, pos_hbm, shift_hbm, wqkv_hbm, sharp_hbm, mex_hbm, gain_hbm, int_hbm, off_hbm, wup_hbm, wdn_hbm, cot_hbm,
    mixed_ref, gfin,
    f_ref, pos_ref, shift_ref, gain_ref, off_ref, sharp_ref, wup_ref, wdn_ref, cot_ref,
    zs, arr, arrf, xin, xa, own4, all4, own_sharp, all_sharp, xrow, nall, back, wup_t, wdn_t, low, xt, ctt, mlp, rs, xs, xr, cross,
    g32, gs16, crecv, db16, drecv, hb16, nr, hb2, nr2, cb16, fr,
    zss, zrs, tss, trs, wss, wrs, css, crs, sss, srs, ass, ars, mss, mrs, gss, grs, dss, drs, oss, ors, los,
):
    dp = lax.axis_index("dp")
    table = lax.axis_index("table")
    tensor = lax.axis_index("tensor")
    z, core = table // 2, lax.rem(table, 2)
    hi, y = tensor // 4, lax.rem(tensor, 4)
    sibling = table + 1 - 2 * core

    def around(k):
        return lax.rem(table + TABLE + k, TABLE)

    def tensor_at(k):
        return lax.rem(tensor + k, TENSOR)

    def settle(*groups):
        for group in groups:
            for copy in group:
                copy.wait_send()

    barrier = pltpu.get_barrier_semaphore()
    for k in FAR_FIRST:
        pl.semaphore_signal(barrier, inc=1, device_id={"table": around(k)}, device_id_type=MESH)
    for k in range(1, TENSOR):
        pl.semaphore_signal(barrier, inc=1, device_id={"tensor": tensor_at(k)}, device_id_type=MESH)
    pl.semaphore_signal(barrier, inc=1, device_id={"dp": 1 - dp}, device_id_type=MESH)

    loads = []
    for hbm, ref in (
        (f_hbm, f_ref), (wqkv_hbm, own4.at[0:3]), (mex_hbm, own4.at[3]), (sharp_hbm, sharp_ref), (wup_hbm, wup_ref),
        (wdn_hbm, wdn_ref), (int_hbm, low.at[0:64]), (cot_hbm, cot_ref), (pos_hbm, pos_ref), (shift_hbm, shift_ref),
        (gain_hbm, gain_ref), (off_hbm, off_ref),
    ):
        copy = pltpu.make_async_copy(hbm, ref, los.at[len(loads)])
        copy.start()
        loads.append(copy)

    loads[0].wait()
    zs[...] = f_ref[...].T
    arr[TABLE - 1] = zs[pl.ds(pl.multiple_of(16 * table, 16), 16), :]
    for copy in loads[1:4]:
        copy.wait()
    own_sharp[...] = jnp.broadcast_to(sharp_ref[...], own_sharp.shape)

    pl.semaphore_wait(barrier, TABLE - 1 + TENSOR - 1 + 1)

    ring = (1, 3, 2)

    def at(h, k):
        return 4 * lax.rem(hi + h, 2) + lax.rem(y + 4 + k, 4)

    def shard(block, count, owner):
        return all4.at[pl.ds(2 * core + block, count), pl.ds(pl.multiple_of(64 * owner, 64), 64), :]

    all4[pl.ds(2 * core, 2), pl.ds(pl.multiple_of(64 * tensor, 64), 64), :] = own4[pl.ds(2 * core, 2)]
    all_sharp[tensor] = own_sharp[...]
    weights, sharps = [], []

    def spread(block, count, owner, n, to):
        copy = remote(shard(block, count, owner), shard(block, count, owner), wss.at[n], wrs.at[n], tensor=to)
        copy.start()
        weights.append(copy)

    spread(0, 2, tensor, 0, at(1, 0))
    for k in ring:
        spread(0, 2, tensor, k, at(0, k))

    for k in FAR_FIRST:
        rows = zs.at[pl.ds(pl.multiple_of(16 * around(k), 16), 16), :]
        remote(rows, arr.at[k - 1], zss.at[0], zrs.at[0], table=around(k)).start()
    all_rows = remote(arr.at[0 : TABLE - 1], arr.at[0 : TABLE - 1], zss.at[0], zrs.at[0], table=around(1))
    for k in range(1, TENSOR):
        copy = remote(own_sharp, all_sharp.at[tensor], sss.at[k], srs.at[k], tensor=tensor_at(k))
        copy.start()
        sharps.append(copy)

    over = []

    def hand_over(owner):
        n = len(over)
        copy = remote(shard(0, 2, owner), shard(0, 2, owner), css.at[n], crs.at[n], table=sibling)
        copy.start()
        over.append(copy)

    hand_over(tensor)

    for copy in loads[4:]:
        copy.wait()
    wup_t[...] = wup_ref[...].T
    wdn_t[...] = wdn_ref[...].T
    low[64:128] = (iota((64, 512), 1) == 64 * tensor + iota((64, 512), 0)).astype(F32).astype(BF16)

    def backward(i, carry):
        rows = cot_ref[pl.ds(pl.multiple_of(128 * i, 128), 128), :]
        back[i] = nt(wdn_ref[...], rows)
        ctt[i] = nt(low[64:128], rows)
        return carry

    lax.fori_loop(0, TENSOR, backward, 0)
    g32[...] = jnp.zeros_like(g32)

    lane = iota((1, 128), 1)
    left = lane < 64
    hot = (iota((64, 64), 0) == pos_ref[...]).astype(F32).astype(BF16)
    j = iota((64, 64), 1)
    source = 2 * lax.rem(table - lax.rem(j, 32) - 1 + TABLE, TABLE) + j // 32
    place = nn(hot, (iota((64, 64), 0) == source).astype(F32).astype(BF16)).astype(BF16)
    shift = shift_ref[...]
    shift = jnp.concatenate([shift, shift], axis=1)

    weights[0].wait_recv()
    for k in ring:
        spread(0, 1, at(1, 0), 4 + k, at(0, k))
    hand_over(at(1, 0))
    for n, k in enumerate(ring):
        weights[1 + n].wait_recv()
        spread(1, 1, at(0, -k), 8 + k, at(1, 0))
        hand_over(at(0, -k))

    all_rows.wait_recv()
    arrf[...] = arr[...].astype(F32)
    for i in range(TENSOR):
        a, b = arrf[:, 2 * i, :], arrf[:, 2 * i + 1, :]
        even = jnp.where(left, a, pltpu.roll(b, 64, 1))
        odd = jnp.where(left, pltpu.roll(a, 64, 1), b)
        rows = jnp.concatenate([even, odd], axis=0).astype(BF16)
        xin[i] = (nn(place, rows) + shift).astype(BF16)
    to_tensor = []
    for k in range(1, TENSOR):
        copy = remote(xin.at[tensor_at(k)], xa.at[tensor], tss.at[k], trs.at[k], tensor=tensor_at(k))
        copy.start()
        to_tensor.append(copy)
    xa[tensor] = xin[tensor]

    def columns(i, carry):
        t = xin[i].astype(F32).T
        xt[i] = jnp.concatenate([t[0:64], t[64:128]], axis=1)
        return carry
    lax.fori_loop(0, TENSOR, columns, 0)
    term = ctt[...] * xt[...]
    ctt[...] = term
    bias = jnp.sum(jnp.sum(term, axis=0), axis=1, keepdims=True)

    for n, k in enumerate(ring):
        weights[4 + n].wait_recv()
        weights[7 + n].wait_recv()
        hand_over(at(1, -k))
    for copy in to_tensor + sharps:
        copy.wait_recv()

    for i in range(4):
        a, b = xa[2 * i].astype(F32), xa[2 * i + 1].astype(F32)
        span = slice(128 * i, 128 * i + 128)
        xrow[0:64, span] = jnp.where(left, a, pltpu.roll(b, 64, 1)).astype(BF16)
        xrow[64:128, span] = jnp.where(left, pltpu.roll(a, 64, 1), b).astype(BF16)
    for copy in over:
        copy.wait_recv()

    x = xrow[...]
    spans = [slice(128 * i, 128 * i + 128) for i in range(4)]
    same = iota((128, 128), 0) // 64 == iota((128, 128), 1) // 64
    same_head = same.astype(F32).astype(BF16)
    query, key, value = nt(x, all4[0]), nt(x, all4[1]), nt(x, all4[2])
    pairs = jnp.concatenate([query[:, span] for span in spans] + [key[:, span] for span in spans], axis=0)
    pairs = pairs * lax.rsqrt(nn((pairs * pairs).astype(BF16), same_head) * (1.0 / 64) + EPS)
    ones = jnp.concatenate([jnp.where(left, 1.0, jnp.zeros((128, 128), F32)), jnp.where(left, jnp.zeros((128, 128), F32), 1.0)], axis=0)
    heads = []
    for i in range(4):
        q, k = pairs[128 * i : 128 * i + 128], pairs[512 + 128 * i : 640 + 128 * i].astype(BF16)
        both = jnp.concatenate([jnp.where(left, q, 0.0), jnp.where(left, 0.0, q)], axis=0).astype(BF16)
        scores = nt(both, k)
        e = [
            jnp.where(same, jnp.exp(scores[128 * s : 128 * s + 128] * (all_sharp[2 * i + s, 0:1, :] * (1.0 / 64))), 0.0)
            for s in range(2)
        ]
        v = value[:, spans[i]]
        v = jnp.concatenate([jnp.where(left, v, 0.0), jnp.where(left, 0.0, v)], axis=0)
        v = jnp.concatenate([v, ones], axis=1).astype(BF16)
        o = nn(jnp.concatenate(e, axis=1).astype(BF16), v)
        heads.append((o[:, 0:128] / o[:, 128:256]).astype(BF16))
    summed = nn(jnp.concatenate(heads, axis=1), all4[3]) + x.astype(F32)
    mean = jnp.mean(summed * summed, axis=1, keepdims=True)
    nall[tensor] = (summed * lax.rsqrt(mean + EPS) * gain_ref[...]).astype(BF16)

    def pass_on(rows, n, to):
        return remote(rows, rows, ass.at[n], ars.at[n], tensor=to)

    pass_on(nall.at[tensor], 0, at(1, 0)).start()
    for k in ring:
        pass_on(nall.at[tensor], k, at(0, k)).start()

    settle([all_rows], to_tensor, weights, sharps, over)
    off = jnp.sum(jnp.where(iota((64, 64), 0) == iota((64, 64), 1), off_ref[...], 0.0), axis=1, keepdims=True)

    def chunk(r, carry):
        m = lax.rem(r + 1, 3)
        dy = (r + 6) // 8 * (1 + 2 * m - 3 * (m // 2))
        dh = r // 5 + (r + 7) // 8 - (r + 6) // 8
        i = at(dh, -dy)
        first, second = nall.at[i, 0:64], nall.at[i, 64:128]

        @pl.when(r == 1)
        def _():
            pass_on(nall.at[i], 0, at(1, 0)).wait_recv()
            for k in ring:
                pass_on(first, 4 + k, at(0, k)).start()

        @pl.when(jnp.logical_and(r >= 2, r <= 4))
        def _():
            pass_on(nall.at[i], dy, at(1, 0)).wait_recv()
            pass_on(second, 8 + dy, at(1, 0)).start()

        @pl.when(r >= 5)
        def _():
            pass_on(first, 4 + dy, at(1, 0)).wait_recv()
            pass_on(second, 8 + dy, at(1, 0)).wait_recv()

        n = nall[i]
        h = nt(wup_t[...], n)
        sg = 1.0 / (1.0 + jnp.exp(-h))
        act = (h * sg).astype(BF16)
        slope = (back[i] * sg * (1.0 + h * (1.0 - sg))).astype(BF16)
        mlp[i] = nn(wdn_t[...], act).astype(BF16)
        rows = cot_ref[pl.ds(pl.multiple_of(128 * i, 128), 128), :]
        down = nn(act, rows)
        up = nt(n.T, slope)
        side = nn(ctt[i].astype(BF16), n)
        for t in range(4):
            span = slice(128 * t, 128 * t + 128)
            g32[512 * t : 512 * t + 512] += up[:, span]
            g32[2048 + 512 * t : 2560 + 512 * t] += down[:, span]
            g32[4096 + 64 * t : 4160 + 64 * t] += side[:, span]
        c = nt(low[...], n)
        cross[i] = xt[i] * (c[0:64] + off) + c[64:128]
        return carry

    lax.fori_loop(0, TENSOR, chunk, 0)
    g32[4352:4416] = jnp.broadcast_to(bias, (64, 128))

    def rows_of(c, zz, d, count):
        zz = lax.rem(zz + 2 * Z, Z)
        start = HALF * c + CLASS * lax.rem(zz, 4) + CHUNK * (zz // 4) + PIECE * d
        return pl.ds(pl.multiple_of(start, 16), count)

    def half(d):
        return pl.ds(pl.multiple_of(PIECE * d, 16), PIECE)

    steps = (8, 4, 12, 0)
    near_z = (1, -1, 4 * core - 2)
    near_by = (2, -2, 8 * core - 4)
    cores, twins, near, far = [], {}, {}, {}
    for s, k in enumerate(steps):
        for j, d in enumerate((1, -1, 2 - 4 * core, 0)):
            gs16[4 * s + j] = g32[rows_of(1 - core, z + d + k, 0, CHUNK), :].astype(BF16)
        four = pl.ds(4 * s, 4)
        copy = remote(gs16.at[four], crecv.at[four], css.at[8 + s], crs.at[8 + s], table=sibling)
        copy.start()
        cores.append(copy)

    def columns_of(h, k):
        return pl.ds(pl.multiple_of(64 * at(h, k), 64), 64)

    terms = []
    for n, k in enumerate(ring):
        for h in range(2):
            copy = remote(
                mlp.at[:, columns_of(h, k), :], rs.at[2 * n + h], mss.at[2 * n + h], mrs.at[2 * n + h], tensor=at(0, k)
            )
            copy.start()
            terms.append(copy)

    for s, k in enumerate(steps):
        cores[s].wait_recv()
        if s == 2:
            for i in range(3):
                both = g32[rows_of(core, z + near_z[i] + k, 0, CHUNK), :] + crecv[8 + i].astype(F32)
                hb2[i] = both.astype(BF16)
                near[6 + i] = remote(hb2.at[i], nr2.at[i], gss.at[6 + i], grs.at[6 + i], table=around(near_by[i]))
                near[6 + i].start()
            continue
        for j, d in enumerate(near_z + (0,)):
            n = 4 * s + j
            theirs = g32[rows_of(core, z + d + k, 1 - dp, PIECE), :] + crecv[n, half(1 - dp), :].astype(F32)
            db16[n] = theirs.astype(BF16)
        four = pl.ds(4 * s, 4)
        twins[s] = remote(db16.at[four], drecv.at[four], dss.at[s], drs.at[s], dp=1 - dp)
        twins[s].start()

    def ours(n, zz):
        total = g32[rows_of(core, zz, dp, PIECE), :] + crecv[n, half(dp), :].astype(F32)
        return total + drecv[n].astype(F32)

    def send_near(s):
        twins[s].wait_recv()
        for i in range(3):
            n = 3 * s + i
            hb16[n] = ours(4 * s + i, z + near_z[i] + steps[s]).astype(BF16)
            near[n] = remote(hb16.at[n], nr.at[n], gss.at[n], grs.at[n], table=around(near_by[i]))
            near[n].start()

    def four_chips(s):
        total = ours(4 * s + 3, z + steps[s])
        for n in range(3 * s, 3 * s + 3):
            near[n].wait_recv()
            total = total + nr[n].astype(F32)
        return total

    def far_on(s, total):
        cb16[s] = total.astype(BF16)
        far[s] = remote(cb16.at[s], fr.at[s], gss.at[12 + s], grs.at[12 + s], table=around(2 * steps[s]))
        far[s].start()

    send_near(0)
    for n in range(6, 9):
        near[n].wait_recv()

    def third(d):
        total = g32[rows_of(core, z + steps[2], d, PIECE), :] + crecv[11, half(d), :].astype(F32)
        for i in range(3):
            total = total + nr2[i, half(d), :].astype(F32)
        return total

    db16[11] = third(1 - dp).astype(BF16)
    twins[2] = remote(db16.at[11], drecv.at[11], dss.at[2], drs.at[2], dp=1 - dp)
    twins[2].start()
    send_near(1)
    far_on(0, four_chips(0))
    twins[2].wait_recv()
    far_on(2, third(dp) + drecv[11].astype(F32))
    send_near(3)
    far_on(1, four_chips(1))
    for copy in terms:
        copy.wait_recv()

    def term_sum(i, h):
        total = mlp[i, columns_of(h, 0), :].astype(F32)
        for n in range(3):
            total = total + rs[2 * n + h, i].astype(F32)
        return total

    def partner_terms(i, carry):
        xs[i] = term_sum(i, 1).astype(BF16)
        return carry

    lax.fori_loop(0, TENSOR, partner_terms, 0)
    terms.append(remote(xs, xr, mss.at[6], mrs.at[6], tensor=at(1, 0)))
    terms[6].start()
    total = four_chips(3)
    for n in range(3):
        far[n].wait_recv()
        total = total + fr[n].astype(F32)
    gfin[rows_of(core, z, dp, PIECE), :] = total.astype(BF16)

    back_far, back_near, back_dp, across = {}, {}, {}, {}

    def send_same(zz, send, recv, n, **device):
        block = gfin.at[rows_of(core, zz, dp, PIECE), :]
        copy = remote(block, block, send.at[n], recv.at[n], **device)
        copy.start()
        return copy

    def owner(s, i):
        return z - steps[s] - (near_z + (0,))[i]

    def to_dp(s, i):
        back_dp[s, i] = send_same(owner(s, i), dss, drs, 16 + 4 * s + i, dp=1 - dp)

    def to_near(s):
        for i in range(3):
            back_near[s, i] = send_same(owner(s, 3), gss, grs, 18 + 3 * s + i, table=around(near_by[i]))

    def to_core(s, i):
        back_dp[s, i].wait_recv()
        block = gfin.at[rows_of(core, owner(s, i), 0, CHUNK), :]
        across[s, i] = remote(block, block, oss.at[4 * s + i], ors.at[4 * s + i], table=sibling)
        across[s, i].start()

    def from_near(s):
        for i in range(3):
            back_near[s, i].wait_recv()
            to_dp(s, i)

    for s in range(3):
        back_far[s] = send_same(z, gss, grs, 15 + s, table=around(2 * steps[s]))
    to_near(3)
    to_dp(3, 3)
    settle(cores, twins.values(), near.values(), far.values(), terms[:6])
    pass_on(nall.at[tensor], 0, at(1, 0)).wait_send()
    for k in ring:
        pass_on(nall.at[tensor], k, at(0, k)).wait_send()
        pass_on(nall.at[tensor, 0:64], 4 + k, at(0, k)).wait_send()
        pass_on(nall.at[tensor, 64:128], 8 + k, at(1, 0)).wait_send()
    from_near(3)
    to_core(3, 3)
    for s in (1, 2):
        back_far[s].wait_recv()
        to_near(s)
        to_dp(s, 3)
    for i in range(3):
        to_core(3, i)
    back_far[0].wait_recv()
    to_near(0)
    to_dp(0, 3)
    from_near(1)
    from_near(2)

    terms[6].wait_recv()

    def finish(i, carry):
        own = term_sum(i, 0) + xr[i].astype(F32)
        out = (cross[i] + own).T
        mixed_ref[2 * i] = out[0:64].astype(BF16)
        mixed_ref[2 * i + 1] = out[64:128].astype(BF16)
        return carry

    lax.fori_loop(0, TENSOR, finish, 0)
    from_near(0)
    for s in (1, 2):
        for i in (3, 0, 1, 2):
            to_core(s, i)
    for i in (3, 0, 1, 2):
        to_core(0, i)
    settle(terms[6:], back_far.values(), back_near.values(), back_dp.values())
    for copy in across.values():
        copy.wait_recv()
    settle(across.values())


def write_out(mixed_ref, g_ref, mixed_hbm, gc_hbm, gb_hbm, gu_hbm, gd_hbm, gc, gb, gu, gd, sems):
    copies = []

    def send(ref, hbm):
        copies.append(pltpu.make_async_copy(ref, hbm, sems.at[len(copies)]))
        copies[-1].start()

    send(mixed_ref, mixed_hbm)
    for t in range(4):
        gu[:, 128 * t : 128 * t + 128] = g_ref[512 * t : 512 * t + 512].astype(F32)
    send(gu, gu_hbm)
    for t in range(4):
        gd[:, 128 * t : 128 * t + 128] = g_ref[2048 + 512 * t : 2560 + 512 * t].astype(F32)
    send(gd, gd_hbm)
    for t in range(4):
        gc[:, 128 * t : 128 * t + 128] = g_ref[4096 + 64 * t : 4160 + 64 * t].astype(F32)
    send(gc, gc_hbm)
    gb[...] = g_ref[4352:4416].astype(F32).T[0:1]
    send(gb, gb_hbm)
    for copy in copies:
        copy.wait()


def body(
    fetched_table_entries,
    position_category_number,
    category_shift_vector,
    asker_matcher_content_matrix,
    affinity_sharpness,
    mixer_exit_matrix,
    mixer_rescale_factor,
    interact_matrix,
    interact_offset_vector,
    widening_matrix,
    narrowing_matrix,
    incoming_cotangent,
):
    vmem = pl.BlockSpec(memory_space=pltpu.VMEM)
    operands = (
        jnp.transpose(fetched_table_entries, (0, 2, 1)).reshape(128, 512),
        position_category_number.reshape(1, 64),
        category_shift_vector,
        jnp.transpose(asker_matcher_content_matrix, (1, 2, 0)),
        affinity_sharpness.reshape(1, 1),
        mixer_exit_matrix,
        mixer_rescale_factor.reshape(1, 512),
        interact_matrix.T,
        interact_offset_vector.reshape(1, 64),
        widening_matrix,
        narrowing_matrix,
        incoming_cotangent.reshape(1024, 512),
    )
    dma = pltpu.SemaphoreType.DMA
    scratch = [
        pltpu.VMEM((128, 512), BF16),
        pltpu.VMEM((1, 64), jnp.int32),
        pltpu.VMEM((64, 64), F32),
        pltpu.VMEM((1, 512), F32),
        pltpu.VMEM((1, 64), F32),
        pltpu.VMEM((1, 1), F32),
        pltpu.VMEM((512, 512), BF16),
        pltpu.VMEM((512, 512), BF16),
        pltpu.VMEM((1024, 512), BF16),
        pltpu.VMEM((512, 128), BF16),
        pltpu.VMEM((32, 16, 128), BF16),
        pltpu.VMEM((32, 16, 128), F32),
        pltpu.VMEM((8, 64, 128), BF16),
        pltpu.VMEM((8, 64, 128), BF16),
        pltpu.VMEM((4, 64, 512), BF16),
        pltpu.VMEM((4, 512, 512), BF16),
        pltpu.VMEM((8, 128), F32),
        pltpu.VMEM((8, 8, 128), F32),
        pltpu.VMEM((128, 512), BF16),
        pltpu.VMEM((8, 128, 512), BF16),
        pltpu.VMEM((8, 512, 128), F32),
        pltpu.VMEM((512, 512), BF16),
        pltpu.VMEM((512, 512), BF16),
        pltpu.VMEM((128, 512), BF16),
        pltpu.VMEM((8, 64, 128), F32),
        pltpu.VMEM((8, 64, 128), F32),
        pltpu.VMEM((8, 512, 128), BF16),
        pltpu.VMEM((6, 8, 64, 128), BF16),
        pltpu.VMEM((8, 64, 128), BF16),
        pltpu.VMEM((8, 64, 128), BF16),
        pltpu.VMEM((8, 64, 128), F32),
        pltpu.VMEM((ROWS, 128), F32),
        pltpu.VMEM((16, CHUNK, 128), BF16),
        pltpu.VMEM((16, CHUNK, 128), BF16),
        pltpu.VMEM((16, PIECE, 128), BF16),
        pltpu.VMEM((16, PIECE, 128), BF16),
        pltpu.VMEM((12, PIECE, 128), BF16),
        pltpu.VMEM((12, PIECE, 128), BF16),
        pltpu.VMEM((3, CHUNK, 128), BF16),
        pltpu.VMEM((3, CHUNK, 128), BF16),
        pltpu.VMEM((3, PIECE, 128), BF16),
        pltpu.VMEM((3, PIECE, 128), BF16),
    ]
    for n in (1, 8, 12, 12, 8, 12, 7, 30, 32, 16):
        scratch += [dma((n,)), dma((n,))]
    scratch.append(dma((12,)))
    mixed, grads = pl.pallas_call(
        kernel,
        name="layer",
        out_shape=(pltpu.VMEM((16, 64, 64), BF16), pltpu.VMEM((ROWS, 128), BF16)),
        in_specs=[pl.BlockSpec(memory_space=pltpu.HBM)] * len(operands),
        out_specs=(vmem,) * 2,
        scratch_shapes=scratch,
        compiler_params=pltpu.CompilerParams(
            collective_id=0, has_side_effects=True, vmem_limit_bytes=58 * 2**20
        ),
    )(*operands)
    hbm = pl.BlockSpec(memory_space=pltpu.HBM)
    mixed, cross, bias, up, down = pl.pallas_call(
        write_out,
        name="write_out",
        out_shape=(
            jax.ShapeDtypeStruct((16, 64, 64), BF16),
            jax.ShapeDtypeStruct((64, 512), F32),
            jax.ShapeDtypeStruct((1, 64), F32),
            jax.ShapeDtypeStruct((512, 512), F32),
            jax.ShapeDtypeStruct((512, 512), F32),
        ),
        in_specs=(vmem,) * 2,
        out_specs=(hbm,) * 5,
        scratch_shapes=[
            pltpu.VMEM((64, 512), F32),
            pltpu.VMEM((1, 64), F32),
            pltpu.VMEM((512, 512), F32),
            pltpu.VMEM((512, 512), F32),
            dma((5,)),
        ],
        compiler_params=pltpu.CompilerParams(vmem_limit_bytes=16 * 2**20),
    )(mixed, grads)
    return mixed, cross.T, bias.reshape(64), up, down


def solution(mesh):
    in_specs = (
        P("table", "dp", "tensor"),
        P(),
        P(None, "tensor"),
        P(None, None, "tensor"),
        P("tensor"),
        P("tensor", None),
        P(),
        P(None, "tensor"),
        P("tensor"),
        P(None, "tensor"),
        P("tensor", None),
        P(("dp", "table"), None, None),
    )
    out_specs = (
        P(("dp", "table"), None, "tensor"),
        P(None, "tensor"),
        P("tensor"),
        P(None, "tensor"),
        P("tensor", None),
    )
    return jax.shard_map(body, mesh=mesh, in_specs=in_specs, out_specs=out_specs, check_vma=False)
```
